32 devices in a mesh: groups: 2 (over x), chan: 16 (over z, y, core).
Axes of the slice: x: 2, y: 2, z: 4, core: 2. Of those that a mesh axis runs over, the one named last changes fastest.
Arguments:
- sky_data: bfloat16 [1024, 512, 2, 256], P('groups', 'chan'), parts along dimension 0, may hold values from -1.1953125 to 1.1953125
- beam_gains: bfloat16 [1024, 512, 256], P('groups', 'chan'), parts along dimension 0, may hold values from 0.099609375 to 1
- mixing: float32 [1024, 4], P(('groups', 'chan')), parts along dimension 0, may hold values from -0.25 to 0.25
- noise_levels: int32 [512], P('chan'), may hold values from 1 to 16
- threshold_levels: int32 [4, 2], replicated, may hold values from 1 to 8
- start_sources: float32 [1024, 4, 256], P(('groups', 'chan')), parts along dimension 0, may hold values from -6 to 6
Outputs:
- sources: float32 [1024, 4, 256], P(('groups', 'chan')), parts along dimension 0
The draws below stay inside these ranges and needn't reach their ends.
There are 2 independent parts, one for each index of `groups`. The reference program is written for one: setup_inputs(seed, part) draws one part's arguments, and reference() takes and returns one part's arrays. A program takes and returns all parts, laid end to end along the dimension named above; an argument that names none is the same for every part. Nothing has to cross between parts.
All inputs are finite; a program needn't handle non-finite values.
Results may differ from the reference program's by a relative error of at most 0.025.
Values may be sent and summed in bfloat16 or wider, within the bound.
A program may use at most 128 MiB of HBM per device.

```python
import math
import jax
import jax.numpy as jnp
from jax import lax

CHANNELS = 512
NROW = 512
NCOL = 256
NS = 4
ITERS = 2
N_CHAN = 16


def set_ends(values, own_key, smallest, high):
    extent = values.shape
    spot = [jax.random.randint(jax.random.fold_in(own_key, axis), (), 0, extent[axis]) for axis in range(len(extent))]
    values = values.at[tuple(spot)].set(smallest)
    longest = extent.index(max(extent))
    spot[longest] = (spot[longest] + 1) % extent[longest]
    return values.at[tuple(spot)].set(high)


def level_of(own_key, shape, shards, low, top_value):
    def one(position, parts):
        draws = jax.random.uniform(jax.random.fold_in(jax.random.fold_in(own_key, 6), position), (parts,), jnp.float32, low / len(shards), top_value / len(shards))
        return jnp.repeat(jnp.exp(draws), shape[position] // parts).reshape((-1,) + (1,) * (len(shape) - position - 1))

    level = one(*shards[0])
    for cut in shards[1:]:
        level = level * one(*cut)
    return level


def bell_draw(rng, dims, scale, most, split=(), kind=jnp.bfloat16):
    drawn = jax.random.normal(rng, dims, jnp.float32) * scale
    if len(split) > 0:
        drawn = level_of(rng, dims, split, -0.22, 0.18) * drawn
    return jnp.clip(drawn, min=-most, max=most).astype(kind)


def setup_inputs(seed: int = 0, part: int = 0) -> dict:
    splits = jax.random.split(jax.random.key(seed), 7)
    part_splits = jax.random.split(jax.random.fold_in(splits[6], part), 7)
    sky_data = bell_draw(part_splits[0], (NROW, CHANNELS, 2, NCOL), 0.2, 1.1953125, ((1, 16),))
    beam_gains = jnp.clip(jnp.exp(math.log(1.0) - 2.306499 * jax.random.uniform(part_splits[1], (NROW, CHANNELS, NCOL), jnp.float32) ** level_of(part_splits[1], (NROW, CHANNELS, NCOL), ((1, 16),), -0.2, 0.2)), 0.099609375, 1.0).astype(jnp.bfloat16)
    mixing = bell_draw(part_splits[2], (CHANNELS, NS), CHANNELS ** -0.5, 0.25, ((0, 16),), jnp.float32)
    noise_levels = set_ends(jax.random.randint(splits[3], (CHANNELS,), 1, 17), jax.random.fold_in(splits[3], 1), 1, 16).astype(jnp.int32)
    threshold_levels = set_ends(jax.random.randint(splits[4], (NS, 2), 1, 9), jax.random.fold_in(splits[4], 1), 1, 8).astype(jnp.int32)
    start_sources = bell_draw(part_splits[5], (NROW, NS, NCOL), 1.0, 6.0, ((0, 16),), jnp.float32)
    return {"sky_data": sky_data, "beam_gains": beam_gains, "mixing": mixing, "noise_levels": noise_levels, "threshold_levels": threshold_levels, "start_sources": start_sources}


def dft_tables(length):
    positions = jnp.arange(length, dtype=jnp.int32)
    angles = (positions[:, None] * positions[None, :] % length).astype(jnp.float32) * (2.0 * math.pi / length)
    norm_factor = 1.0 / math.sqrt(length)
    return ((jnp.cos(angles) * norm_factor).astype(jnp.bfloat16), (-jnp.sin(angles) * norm_factor).astype(jnp.bfloat16))

def column_part(rounded, col_cat):
    row_count, source_count, col_count = rounded.shape
    product = jnp.dot(rounded.reshape(row_count * source_count, col_count), col_cat, preferred_element_type=jnp.float32)
    return product.astype(jnp.bfloat16).reshape(row_count, source_count * 2 * col_count)

def combine_forward(real_prod, imag_prod, source_count, col_count):
    real_prod = real_prod.reshape(real_prod.shape[0], source_count, 2, col_count)
    imag_prod = imag_prod.reshape(imag_prod.shape[0], source_count, 2, col_count)
    real_out = real_prod[:, :, 0] - imag_prod[:, :, 1]
    imag_out = real_prod[:, :, 1] + imag_prod[:, :, 0]
    return jnp.stack([real_out, imag_out], axis=2)

def inverse_rows(row_real, row_imag, packed_grad, col_back, source_count, col_count):
    real_prod = jnp.dot(row_real, packed_grad, preferred_element_type=jnp.float32)
    imag_prod = jnp.dot(row_imag, packed_grad, preferred_element_type=jnp.float32)
    real_prod = real_prod.reshape(real_prod.shape[0], source_count, 2, col_count)
    imag_prod = imag_prod.reshape(imag_prod.shape[0], source_count, 2, col_count)
    real_out = real_prod[:, :, 0] + imag_prod[:, :, 1]
    imag_out = real_prod[:, :, 1] - imag_prod[:, :, 0]
    joined = jnp.concatenate([real_out, imag_out], axis=-1).astype(jnp.bfloat16)
    result = jnp.dot(joined.reshape(-1, 2 * col_count), col_back, preferred_element_type=jnp.float32)
    return result.reshape(real_prod.shape[0], source_count, col_count)

def block_gradient(fourier, data_block, beam_block, mix_block, level_block):
    predicted = jnp.einsum('ct,ktzl->kczl', mix_block.astype(jnp.float32), fourier.astype(jnp.float32))
    beam_gain = beam_block.astype(jnp.float32)[:, :, None, :]
    residual = data_block.astype(jnp.float32) - beam_gain * predicted
    weight = level_block.astype(jnp.float32) * 0.25
    weighted = weight[None, :, None, None] * beam_gain * residual
    summed = jnp.einsum('cs,kczl->kszl', mix_block.astype(jnp.float32), weighted)
    return summed.astype(jnp.bfloat16)

def smooth_cols(values, spacing):
    padded = jnp.pad(values, ((0, 0), (0, 0), (spacing, spacing)))
    return (padded[..., :-2 * spacing] + 2.0 * padded[..., spacing:-spacing] + padded[..., 2 * spacing:]) * 0.25

def smooth_whole(values, spacing):
    padded = jnp.pad(values, ((spacing, spacing), (0, 0), (0, 0)))
    row_done = (padded[:-2 * spacing] + 2.0 * padded[spacing:-spacing] + padded[2 * spacing:]) * 0.25
    return smooth_cols(row_done, spacing)

def shrink(values, bound_value):
    return values - jnp.clip(values, -bound_value, bound_value)

def combine_scales(updated, smooth_one, coarse, fine_bound, coarse_bound):
    return coarse + shrink(smooth_one - coarse, coarse_bound) + shrink(updated - smooth_one, fine_bound)

def reference(sky_data, beam_gains, mixing, noise_levels, threshold_levels, start_sources):
    row_real, row_imag = dft_tables(NROW)
    col_real, col_imag = dft_tables(NCOL)
    col_cat = jnp.concatenate([col_real, col_imag], axis=1)
    col_back = jnp.concatenate([col_real, col_imag], axis=0)
    bounds = threshold_levels.astype(jnp.float32) * 0.05
    fine_bound = bounds[:, 0][:, None]
    coarse_bound = bounds[:, 1][:, None]
    block_size = CHANNELS // N_CHAN
    sources = start_sources
    for iteration in range(ITERS):
        rounded = sources.astype(jnp.bfloat16)
        packed = column_part(rounded, col_cat)
        fourier = combine_forward(jnp.dot(row_real, packed, preferred_element_type=jnp.float32), jnp.dot(row_imag, packed, preferred_element_type=jnp.float32), NS, NCOL)

        def add_block(block_index, running):
            offset = (block_index * block_size).astype(jnp.int32)
            data_block = lax.dynamic_slice_in_dim(sky_data, offset, block_size, 1)
            beam_block = lax.dynamic_slice_in_dim(beam_gains, offset, block_size, 1)
            mix_block = lax.dynamic_slice_in_dim(mixing, offset, block_size, 0)
            level_block = lax.dynamic_slice_in_dim(noise_levels, offset, block_size, 0)
            grad_block = block_gradient(fourier, data_block, beam_block, mix_block, level_block)
            packed_grad = grad_block.reshape(NROW, NS * 2 * NCOL)
            return running + inverse_rows(row_real, row_imag, packed_grad, col_back, NS, NCOL)
        gradient = lax.fori_loop(0, N_CHAN, add_block, jnp.zeros((NROW, NS, NCOL), jnp.float32))
        updated = sources + gradient
        smooth_one = smooth_whole(updated, 1)
        coarse = smooth_whole(smooth_one, 2)
        sources = combine_scales(updated, smooth_one, coarse, fine_bound, coarse_bound)
    return sources
```

```python
import functools
import math

import jax
import jax.numpy as jnp
import ml_dtypes
import numpy as np
from jax import lax
from jax.experimental import pallas as pl
from jax.experimental.pallas import tpu as pltpu
from jax.sharding import PartitionSpec as P

ITERS = 2


def padded_2(cells, sides, width):
    for axis, dim in sides:
        count = lax.axis_size(axis)
        ends = count - 1
        head = lax.slice_in_dim(cells, 0, width, axis=dim)
        tail = lax.slice_in_dim(cells, cells.shape[dim] - width, cells.shape[dim], axis=dim)
        cells = jnp.concatenate(
            [
                lax.ppermute(tail, axis, [(i, (i + 1) % count) for i in range(ends)]),
                cells,
                lax.ppermute(head, axis, [((i + 1) % count, i) for i in range(ends)]),
            ],
            axis=dim,
        )
    return cells


def dft_tables(length):
    positions = jnp.arange(length, dtype=jnp.int32)
    angles = (positions[:, None] * positions[None, :] % length).astype(jnp.float32) * (
        2.0 * math.pi / length
    )
    norm_factor = 1.0 / math.sqrt(length)
    return (
        (jnp.cos(angles) * norm_factor).astype(jnp.bfloat16),
        (-jnp.sin(angles) * norm_factor).astype(jnp.bfloat16),
    )


def column_part(rounded, col_cat):
    row_count, source_count, col_count = rounded.shape
    product = jnp.dot(
        rounded.reshape(row_count * source_count, col_count),
        col_cat,
        preferred_element_type=jnp.float32,
    )
    return product.astype(jnp.bfloat16).reshape(row_count, source_count * 2 * col_count)


def combine_forward(real_prod, imag_prod, source_count, col_count):
    real_prod = real_prod.reshape(real_prod.shape[0], source_count, 2, col_count)
    imag_prod = imag_prod.reshape(imag_prod.shape[0], source_count, 2, col_count)
    real_out = real_prod[:, :, 0] - imag_prod[:, :, 1]
    imag_out = real_prod[:, :, 1] + imag_prod[:, :, 0]
    return jnp.stack([real_out, imag_out], axis=2)


def inverse_rows(row_real, row_imag, packed_grad, col_back, source_count, col_count):
    real_prod = jnp.dot(row_real, packed_grad, preferred_element_type=jnp.float32)
    imag_prod = jnp.dot(row_imag, packed_grad, preferred_element_type=jnp.float32)
    real_prod = real_prod.reshape(real_prod.shape[0], source_count, 2, col_count)
    imag_prod = imag_prod.reshape(imag_prod.shape[0], source_count, 2, col_count)
    real_out = real_prod[:, :, 0] + imag_prod[:, :, 1]
    imag_out = real_prod[:, :, 1] - imag_prod[:, :, 0]
    joined = jnp.concatenate([real_out, imag_out], axis=-1).astype(jnp.bfloat16)
    result = jnp.dot(
        joined.reshape(-1, 2 * col_count), col_back, preferred_element_type=jnp.float32
    )
    return result.reshape(real_prod.shape[0], source_count, col_count)


def block_gradient(fourier, data_block, beam_block, mix_block, level_block):
    predicted = jnp.einsum("ct,ktzl->kczl", mix_block, fourier)
    beam_gain = beam_block.astype(jnp.float32)[:, :, None, :]
    residual = data_block.astype(jnp.float32) - beam_gain * predicted
    weight = level_block.astype(jnp.float32) * 0.25
    weighted = weight[None, :, None, None] * beam_gain * residual
    summed = jnp.einsum("cs,kczl->kszl", mix_block, weighted)
    return summed.astype(jnp.bfloat16)


def smooth_rows(padded, spacing, row_count):
    return (
        padded[0:row_count]
        + 2.0 * padded[spacing : spacing + row_count]
        + padded[2 * spacing : 2 * spacing + row_count]
    ) * 0.25


def smooth_cols(values, spacing):
    padded = jnp.pad(values, ((0, 0), (0, 0), (spacing, spacing)))
    return (
        padded[..., : -2 * spacing]
        + 2.0 * padded[..., spacing:-spacing]
        + padded[..., 2 * spacing :]
    ) * 0.25


def shrink(values, bound_value):
    return values - jnp.clip(values, -bound_value, bound_value)


def combine_scales(updated, smooth_one, coarse, fine_bound, coarse_bound):
    return (
        coarse
        + shrink(smooth_one - coarse, coarse_bound)
        + shrink(updated - smooth_one, fine_bound)
    )


def plain_body(sky_data, beam_gains, mixing, noise_levels, threshold_levels, start_sources):
    strip_rows, source_count, col_count = start_sources.shape
    full_rows = strip_rows * lax.axis_size("chan")
    row_real, row_imag = dft_tables(full_rows)
    col_real, col_imag = dft_tables(col_count)
    col_cat = jnp.concatenate([col_real, col_imag], axis=1)
    col_back = jnp.concatenate([col_real, col_imag], axis=0)
    bounds = threshold_levels.astype(jnp.float32) * 0.05
    fine_bound = bounds[:, 0][:, None]
    coarse_bound = bounds[:, 1][:, None]
    sources = start_sources
    for iteration in range(ITERS):
        rounded = sources.astype(jnp.bfloat16)
        gathered = lax.all_gather(rounded, "chan", axis=0, tiled=True)
        packed = column_part(gathered, col_cat)
        fourier = combine_forward(
            jnp.dot(row_real, packed, preferred_element_type=jnp.float32),
            jnp.dot(row_imag, packed, preferred_element_type=jnp.float32),
            source_count,
            col_count,
        )
        grad_local = block_gradient(fourier, sky_data, beam_gains, mixing, noise_levels)
        packed_grad = grad_local.reshape(full_rows, source_count * 2 * col_count)
        gradient = lax.psum_scatter(
            inverse_rows(row_real, row_imag, packed_grad, col_back, source_count, col_count),
            "chan",
            scatter_dimension=0,
            tiled=True,
        )
        updated = sources + gradient
        fine_pad = padded_2(updated, (("chan", 0),), 1)
        smooth_one = smooth_cols(smooth_rows(fine_pad, 1, strip_rows), 1)
        coarse_pad = padded_2(smooth_one, (("chan", 0),), 2)
        coarse = smooth_cols(smooth_rows(coarse_pad, 2, strip_rows), 2)
        sources = combine_scales(updated, smooth_one, coarse, fine_bound, coarse_bound)
    return sources


BF16 = jnp.bfloat16
F32 = jnp.float32
VMEM_LIMIT = 56 * 1024 * 1024
PAIRS = [(s, t) for s in range(4) for t in range(s, 4)]
PAIR_OF = {}
for number, (first, second) in enumerate(PAIRS):
    PAIR_OF[first, second] = number
    PAIR_OF[second, first] = number


def host_tables(length):
    positions = np.arange(length)
    angles = (positions[:, None] * positions[None, :] % length) * (2.0 * math.pi / length)
    norm_factor = 1.0 / math.sqrt(length)
    return (
        (np.cos(angles) * norm_factor).astype(np.float32).astype(ml_dtypes.bfloat16),
        (-np.sin(angles) * norm_factor).astype(np.float32).astype(ml_dtypes.bfloat16),
    )


def smooth_window(x, first_row, row_total, fine, coarse_bound):
    height, width = x.shape
    rows = lax.broadcasted_iota(jnp.int32, (height, width), 0) + first_row
    lanes = lax.broadcasted_iota(jnp.int32, (height, width), 1)
    inside = (rows >= 0) & (rows < row_total)

    def smooth(v, d):
        v = 0.25 * (pltpu.roll(v, d, 0) + 2.0 * v + pltpu.roll(v, height - d, 0))
        left = jnp.where(lanes >= d, pltpu.roll(v, d, 1), 0.0)
        right = jnp.where(lanes < width - d, pltpu.roll(v, width - d, 1), 0.0)
        return 0.25 * (left + 2.0 * v + right)

    c1 = jnp.where(inside, smooth(x, 1), 0.0)
    c2 = smooth(c1, 2)
    d1 = c1 - c2
    d0 = x - c1
    result = c2 + (d1 - jnp.clip(d1, -coarse_bound, coarse_bound)) + (d0 - jnp.clip(d0, -fine, fine))
    return result[8 : height - 8]


def step_kernel(
    last, s_ref, own_ref, d_ref, h_ref, colcat_ref, colback_ref, fwd_ref, bwd_ref, lam_ref, out_ref,
    pst, gst, vb, got_core, acc, got_y, fin, got_z, vall, xpad, halo,
    core_s, core_r, y_s, y_r, z_s, z_r, gz_s, gz_r, gy_s, gy_r, gc_s, gc_r, halo_s, halo_r,
):
    blocks, sources, strip, cols = s_ref.shape
    nrow = blocks * strip
    me = lax.axis_index("chan")
    z, y, c = me // 4, (me // 2) % 2, me % 2

    def index(zz, yy, cc):
        return zz * 4 + yy * 2 + cc

    core_peer = index(z, y, 1 - c)
    y_peer = index(z, 1 - y, c)
    z_peers = [index((z + 1 + i) % 4, y, c) for i in range(3)]
    z_from = [index((z + 3 - i) % 4, y, c) for i in range(3)]
    right, left = (me + 1) % blocks, (me + blocks - 1) % blocks

    barrier = pltpu.get_barrier_semaphore()
    greeted = [core_peer, y_peer] + z_peers + ([left, right] if last else [])
    for peer in greeted:
        pl.semaphore_signal(barrier, inc=1, device_id={"chan": peer}, device_id_type=pl.DeviceIdType.MESH)

    def remote(src, dst, send, recv, peer):
        return pltpu.make_async_remote_copy(
            src_ref=src, dst_ref=dst, send_sem=send, recv_sem=recv,
            device_id={"chan": peer}, device_id_type=pl.DeviceIdType.MESH,
        )

    for t in range(sources):
        rows = s_ref[:, t].reshape(nrow, cols).astype(BF16)
        p = jnp.dot(rows, colcat_ref[...], preferred_element_type=F32)
        pst[0:nrow, t * cols : (t + 1) * cols] = p[:, :cols].astype(BF16)
        pst[nrow:, t * cols : (t + 1) * cols] = p[:, cols:].astype(BF16)

    tile = 128

    @pl.loop(0, nrow // tile)
    def _(kb):
        k0 = pl.multiple_of(kb * tile, tile)
        k1 = pl.multiple_of(nrow + kb * tile, tile)
        for part, start in ((0, k0), (1, k1)):
            q = jnp.dot(fwd_ref[pl.ds(start, tile), :], pst[...], preferred_element_type=F32)
            for s in range(sources):
                g = d_ref[part, s, pl.ds(k0, tile), :].astype(F32)
                for t in range(sources):
                    hh = h_ref[PAIR_OF[s, t], pl.ds(k0, tile), :].astype(F32)
                    g = g - hh * q[:, t * cols : (t + 1) * cols]
                gst[pl.ds(start, tile), s * cols : (s + 1) * cols] = g.astype(BF16)

    pl.semaphore_wait(barrier, len(greeted))

    core_copies, y_copies, z_copies = [], [], []

    def do_core(i):
        zb = (z + 1 + i) % 4
        r0 = pl.multiple_of(zb * tile, tile)
        r1 = pl.multiple_of(nrow + zb * tile, tile)
        ur = jnp.dot(bwd_ref[pl.ds(r0, tile), :], gst[...], preferred_element_type=F32).astype(BF16)
        ui = jnp.dot(bwd_ref[pl.ds(r1, tile), :], gst[...], preferred_element_type=F32).astype(BF16)
        for s in range(sources):
            both = jnp.concatenate([ur[:, s * cols : (s + 1) * cols], ui[:, s * cols : (s + 1) * cols]], axis=1)
            v = jnp.dot(both, colback_ref[...], preferred_element_type=F32)
            vb[i, :, :, s] = v.astype(BF16).reshape(2, 2, strip, cols)
        copy = remote(vb.at[i, :, 1 - c], got_core.at[i], core_s.at[i], core_r.at[i], core_peer)
        copy.start()
        core_copies.append(copy)

    def do_y(i):
        core_copies[i].wait()
        acc[i] = (vb[i, :, c].astype(F32) + got_core[i].astype(F32)).astype(BF16)
        copy = remote(acc.at[i, 1 - y], got_y.at[i], y_s.at[i], y_r.at[i], y_peer)
        copy.start()
        y_copies.append(copy)

    def do_z(i):
        y_copies[i].wait()
        fin[i] = (acc[i, y].astype(F32) + got_y[i].astype(F32)).astype(BF16)
        copy = remote(fin.at[i], got_z.at[i], z_s.at[i], z_r.at[i], z_peers[i])
        copy.start()
        z_copies.append(copy)

    do_core(0)
    do_core(1)
    do_y(0)
    do_core(2)
    do_y(1)
    do_z(0)
    do_core(3)
    do_y(2)
    do_z(1)
    do_y(3)
    do_z(2)
    y_copies[3].wait()
    total = acc[3, y].astype(F32) + got_y[3].astype(F32)
    for i in range(3):
        z_copies[i].wait()
        total = total + got_z[i].astype(F32)

    def bound(s, j):
        return lam_ref[s, j]

    if not last:
        vall[me] = total.astype(BF16)
        gz, gy, gc = [], [], []
        for i in range(3):
            copy = remote(vall.at[me], vall.at[me], gz_s.at[i], gz_r.at[i], z_peers[i])
            copy.start()
            gz.append(copy)

        def to_core(src, j):
            copy = remote(vall.at[src], vall.at[src], gc_s.at[j], gc_r.at[j], core_peer)
            copy.start()
            gc.append(copy)

        held = [me] + z_from
        for j in range(4):
            if j > 0:
                gz[j - 1].wait_recv()
            copy = remote(vall.at[held[j]], vall.at[held[j]], gy_s.at[j], gy_r.at[j], y_peer)
            copy.start()
            gy.append(copy)
            to_core(held[j], j)
        for j in range(4):
            gy[j].wait_recv()
            zz = (z + 4 - j) % 4
            to_core(index(zz, 1 - y, c), 4 + j)
        for copy in gc:
            copy.wait_recv()
        for copy in gz + gy + gc:
            copy.wait_send()
        xpad[:, 0:16] = jnp.zeros((sources, 16, cols), F32)
        xpad[:, nrow + 16 :] = jnp.zeros((sources, 16, cols), F32)

        @pl.loop(0, blocks)
        def _(b):
            xpad[:, pl.ds(pl.multiple_of(16 + b * strip, 16), strip)] = s_ref[b].astype(F32) + vall[b].astype(F32)

        xpad[:, pl.ds(pl.multiple_of(16 + me * strip, 16), strip)] = own_ref[...] + total

        @pl.loop(0, blocks)
        def _(b):
            start = pl.multiple_of(8 + b * strip, 8)
            for s in range(sources):
                x = xpad[s, pl.ds(start, strip + 16), :]
                out_ref[b, s] = smooth_window(x, b * strip - 8, nrow, bound(s, 0), bound(s, 1))
    else:
        mine = s_ref[me]
        vall[me] = total.astype(BF16)
        half = strip // 2
        to_right = remote(vall.at[me, :, half:strip], halo.at[0], halo_s.at[0], halo_r.at[0], right)
        to_left = remote(vall.at[me, :, 0:half], halo.at[1], halo_s.at[1], halo_r.at[1], left)
        to_right.start()
        to_left.start()
        xpad[:, 16 : 16 + strip] = mine + total
        above = s_ref[left, :, half:strip]
        below = s_ref[right, :, 0:half]
        to_right.wait()
        to_left.wait()
        above = above + halo[0].astype(F32)
        below = below + halo[1].astype(F32)
        xpad[:, 0:16] = jnp.where(me > 0, above, 0.0)
        xpad[:, 16 + strip : 32 + strip] = jnp.where(me < blocks - 1, below, 0.0)
        for s in range(sources):
            x = xpad[s, 8 : 24 + strip, :]
            out_ref[s] = smooth_window(x, me * strip - 8, nrow, bound(s, 0), bound(s, 1))


def step(last, s_full, own, dd, hh, tables, lam):
    blocks, sources, strip, cols = s_full.shape
    nrow = blocks * strip
    vm = pl.BlockSpec(memory_space=pltpu.VMEM)
    dma = pltpu.SemaphoreType.DMA
    block = (sources, strip, cols)
    return pl.pallas_call(
        functools.partial(step_kernel, last),
        out_shape=jax.ShapeDtypeStruct(block if last else (blocks,) + block, F32),
        in_specs=[vm] * 8 + [pl.BlockSpec(memory_space=pltpu.SMEM)],
        out_specs=vm,
        scratch_shapes=[
            pltpu.VMEM((2 * nrow, sources * cols), BF16),
            pltpu.VMEM((2 * nrow, sources * cols), BF16),
            pltpu.VMEM((4, 2, 2) + block, BF16),
            pltpu.VMEM((4, 2) + block, BF16),
            pltpu.VMEM((4, 2) + block, BF16),
            pltpu.VMEM((4,) + block, BF16),
            pltpu.VMEM((3,) + block, BF16),
            pltpu.VMEM((3,) + block, BF16),
            pltpu.VMEM((blocks,) + block, BF16),
            pltpu.VMEM((sources, (strip if last else nrow) + 32, cols), F32),
            pltpu.VMEM((2, sources, 16, cols), BF16),
            dma((4,)), dma((4,)), dma((4,)), dma((4,)), dma((3,)), dma((3,)),
            dma((3,)), dma((3,)), dma((4,)), dma((4,)), dma((8,)), dma((8,)),
            dma((2,)), dma((2,)),
        ],
        compiler_params=pltpu.CompilerParams(
            collective_id=1 if last else 0, has_side_effects=True, vmem_limit_bytes=VMEM_LIMIT
        ),
    )(s_full, own, dd, hh, *tables, lam)


def channel_sums(sky_data, beam_gains, mixing, noise_levels):
    weighted = mixing * (noise_levels.astype(F32) * 0.25)[:, None]
    beam = beam_gains.astype(F32)
    gd = (beam[:, :, None, :] * sky_data.astype(F32)).astype(BF16)
    gg = (beam * beam).astype(BF16)
    pair = jnp.stack([weighted[:, s] * mixing[:, t] for s, t in PAIRS], axis=1)
    dd = jnp.einsum("cs,kczl->zskl", weighted.astype(BF16), gd, preferred_element_type=F32)
    hh = jnp.einsum("cp,kcl->pkl", pair.astype(BF16), gg, preferred_element_type=F32)
    return dd.astype(BF16), hh.astype(BF16)


def body(sky_data, beam_gains, mixing, noise_levels, threshold_levels, start_sources):
    strip, sources, cols = start_sources.shape
    blocks = lax.axis_size("chan")
    if blocks != 16 or strip != 32 or sources != 4 or cols % 128:
        return plain_body(sky_data, beam_gains, mixing, noise_levels, threshold_levels, start_sources)
    row_real, row_imag = host_tables(strip * blocks)
    col_real, col_imag = host_tables(cols)
    tables = [
        jnp.asarray(np.concatenate([col_real, col_imag], axis=1)),
        jnp.asarray(np.concatenate([col_real, col_imag], axis=0)),
        jnp.asarray(np.block([[row_real, -row_imag], [row_imag, row_real]])),
        jnp.asarray(np.block([[row_real, row_imag], [-row_imag, row_real]])),
    ]
    lam = threshold_levels.astype(F32) * 0.05
    own = jnp.swapaxes(start_sources, 0, 1)
    s_full = lax.all_gather(own.astype(BF16), "chan", axis=0)
    dd, hh = channel_sums(sky_data, beam_gains, mixing, noise_levels)
    s_full = step(False, s_full, own, dd, hh, tables, lam)
    result = step(True, s_full, own, dd, hh, tables, lam)
    return jnp.swapaxes(result, 0, 1)


def solution(mesh):
    return jax.shard_map(
        body,
        mesh=mesh,
        in_specs=(
            P("groups", "chan", None, None),
            P("groups", "chan", None),
            P(("groups", "chan"), None),
            P("chan"),
            P(),
            P(("groups", "chan"), None, None),
        ),
        out_specs=P(("groups", "chan"), None, None),
        check_vma=False,
    )
```

```python
import functools
import math

import jax
import jax.numpy as jnp
import ml_dtypes
import numpy as np
from jax import lax
from jax.experimental import pallas as pl
from jax.experimental.pallas import tpu as pltpu
from jax.sharding import PartitionSpec as P

ITERS = 2


def padded_2(cells, sides, width):
    for axis, dim in sides:
        count = lax.axis_size(axis)
        ends = count - 1
        head = lax.slice_in_dim(cells, 0, width, axis=dim)
        tail = lax.slice_in_dim(cells, cells.shape[dim] - width, cells.shape[dim], axis=dim)
        cells = jnp.concatenate(
            [
                lax.ppermute(tail, axis, [(i, (i + 1) % count) for i in range(ends)]),
                cells,
                lax.ppermute(head, axis, [((i + 1) % count, i) for i in range(ends)]),
            ],
            axis=dim,
        )
    return cells


def dft_tables(length):
    positions = jnp.arange(length, dtype=jnp.int32)
    angles = (positions[:, None] * positions[None, :] % length).astype(jnp.float32) * (
        2.0 * math.pi / length
    )
    norm_factor = 1.0 / math.sqrt(length)
    return (
        (jnp.cos(angles) * norm_factor).astype(jnp.bfloat16),
        (-jnp.sin(angles) * norm_factor).astype(jnp.bfloat16),
    )


def column_part(rounded, col_cat):
    row_count, source_count, col_count = rounded.shape
    product = jnp.dot(
        rounded.reshape(row_count * source_count, col_count),
        col_cat,
        preferred_element_type=jnp.float32,
    )
    return product.astype(jnp.bfloat16).reshape(row_count, source_count * 2 * col_count)


def combine_forward(real_prod, imag_prod, source_count, col_count):
    real_prod = real_prod.reshape(real_prod.shape[0], source_count, 2, col_count)
    imag_prod = imag_prod.reshape(imag_prod.shape[0], source_count, 2, col_count)
    real_out = real_prod[:, :, 0] - imag_prod[:, :, 1]
    imag_out = real_prod[:, :, 1] + imag_prod[:, :, 0]
    return jnp.stack([real_out, imag_out], axis=2)


def inverse_rows(row_real, row_imag, packed_grad, col_back, source_count, col_count):
    real_prod = jnp.dot(row_real, packed_grad, preferred_element_type=jnp.float32)
    imag_prod = jnp.dot(row_imag, packed_grad, preferred_element_type=jnp.float32)
    real_prod = real_prod.reshape(real_prod.shape[0], source_count, 2, col_count)
    imag_prod = imag_prod.reshape(imag_prod.shape[0], source_count, 2, col_count)
    real_out = real_prod[:, :, 0] + imag_prod[:, :, 1]
    imag_out = real_prod[:, :, 1] - imag_prod[:, :, 0]
    joined = jnp.concatenate([real_out, imag_out], axis=-1).astype(jnp.bfloat16)
    result = jnp.dot(
        joined.reshape(-1, 2 * col_count), col_back, preferred_element_type=jnp.float32
    )
    return result.reshape(real_prod.shape[0], source_count, col_count)


def block_gradient(fourier, data_block, beam_block, mix_block, level_block):
    predicted = jnp.einsum("ct,ktzl->kczl", mix_block, fourier)
    beam_gain = beam_block.astype(jnp.float32)[:, :, None, :]
    residual = data_block.astype(jnp.float32) - beam_gain * predicted
    weight = level_block.astype(jnp.float32) * 0.25
    weighted = weight[None, :, None, None] * beam_gain * residual
    summed = jnp.einsum("cs,kczl->kszl", mix_block, weighted)
    return summed.astype(jnp.bfloat16)


def smooth_rows(padded, spacing, row_count):
    return (
        padded[0:row_count]
        + 2.0 * padded[spacing : spacing + row_count]
        + padded[2 * spacing : 2 * spacing + row_count]
    ) * 0.25


def smooth_cols(values, spacing):
    padded = jnp.pad(values, ((0, 0), (0, 0), (spacing, spacing)))
    return (
        padded[..., : -2 * spacing]
        + 2.0 * padded[..., spacing:-spacing]
        + padded[..., 2 * spacing :]
    ) * 0.25


def shrink(values, bound_value):
    return values - jnp.clip(values, -bound_value, bound_value)


def combine_scales(updated, smooth_one, coarse, fine_bound, coarse_bound):
    return (
        coarse
        + shrink(smooth_one - coarse, coarse_bound)
        + shrink(updated - smooth_one, fine_bound)
    )


def plain_body(sky_data, beam_gains, mixing, noise_levels, threshold_levels, start_sources):
    strip_rows, source_count, col_count = start_sources.shape
    full_rows = strip_rows * lax.axis_size("chan")
    row_real, row_imag = dft_tables(full_rows)
    col_real, col_imag = dft_tables(col_count)
    col_cat = jnp.concatenate([col_real, col_imag], axis=1)
    col_back = jnp.concatenate([col_real, col_imag], axis=0)
    bounds = threshold_levels.astype(jnp.float32) * 0.05
    fine_bound = bounds[:, 0][:, None]
    coarse_bound = bounds[:, 1][:, None]
    sources = start_sources
    for iteration in range(ITERS):
        rounded = sources.astype(jnp.bfloat16)
        gathered = lax.all_gather(rounded, "chan", axis=0, tiled=True)
        packed = column_part(gathered, col_cat)
        fourier = combine_forward(
            jnp.dot(row_real, packed, preferred_element_type=jnp.float32),
            jnp.dot(row_imag, packed, preferred_element_type=jnp.float32),
            source_count,
            col_count,
        )
        grad_local = block_gradient(fourier, sky_data, beam_gains, mixing, noise_levels)
        packed_grad = grad_local.reshape(full_rows, source_count * 2 * col_count)
        gradient = lax.psum_scatter(
            inverse_rows(row_real, row_imag, packed_grad, col_back, source_count, col_count),
            "chan",
            scatter_dimension=0,
            tiled=True,
        )
        updated = sources + gradient
        fine_pad = padded_2(updated, (("chan", 0),), 1)
        smooth_one = smooth_cols(smooth_rows(fine_pad, 1, strip_rows), 1)
        coarse_pad = padded_2(smooth_one, (("chan", 0),), 2)
        coarse = smooth_cols(smooth_rows(coarse_pad, 2, strip_rows), 2)
        sources = combine_scales(updated, smooth_one, coarse, fine_bound, coarse_bound)
    return sources


BF16 = jnp.bfloat16
F32 = jnp.float32
VMEM_LIMIT = 56 * 1024 * 1024
PAIRS = [(s, t) for s in range(4) for t in range(s, 4)]
PAIR_OF = {}
for number, (first, second) in enumerate(PAIRS):
    PAIR_OF[first, second] = number
    PAIR_OF[second, first] = number


def host_tables(length):
    positions = np.arange(length)
    angles = (positions[:, None] * positions[None, :] % length) * (2.0 * math.pi / length)
    norm_factor = 1.0 / math.sqrt(length)
    return (
        (np.cos(angles) * norm_factor).astype(np.float32).astype(ml_dtypes.bfloat16),
        (-np.sin(angles) * norm_factor).astype(np.float32).astype(ml_dtypes.bfloat16),
    )


def smooth_window(x, first_row, row_total, fine, coarse_bound):
    height, width = x.shape
    rows = lax.broadcasted_iota(jnp.int32, (height, width), 0) + first_row
    lanes = lax.broadcasted_iota(jnp.int32, (height, width), 1)
    inside = (rows >= 0) & (rows < row_total)

    def smooth(v, d):
        v = 0.25 * (pltpu.roll(v, d, 0) + 2.0 * v + pltpu.roll(v, height - d, 0))
        left = jnp.where(lanes >= d, pltpu.roll(v, d, 1), 0.0)
        right = jnp.where(lanes < width - d, pltpu.roll(v, width - d, 1), 0.0)
        return 0.25 * (left + 2.0 * v + right)

    c1 = jnp.where(inside, smooth(x, 1), 0.0)
    c2 = smooth(c1, 2)
    d1 = c1 - c2
    d0 = x - c1
    result = c2 + (d1 - jnp.clip(d1, -coarse_bound, coarse_bound)) + (d0 - jnp.clip(d0, -fine, fine))
    return result[8 : height - 8]


def step_kernel(
    last, s_ref, own_ref, d_ref, h_ref, colcat_ref, colback_ref, fwd_ref, bwd_ref, lam_ref, *rest
):
    if last:
        (out_ref,), rest = rest[:1], rest[1:]
        dsum_ref, hsum_ref, got_d, got_h = d_ref, h_ref, None, None
    else:
        (out_ref, dsum_ref, hsum_ref), rest = rest[:3], rest[3:]
        (got_d, got_h), rest = rest[:2], rest[2:]
    (
    qst, pst, gst, vb, got_core, acc, got_y, fin, got_z, vall, xpad, halo,
    core_s, core_r, y_s, y_r, z_s, z_r, gz_s, gz_r, gy_s, gy_r, gc_s, gc_r, halo_s, halo_r, half_s, half_r,
    ) = rest
    blocks, sources, strip, cols = s_ref.shape
    nrow = blocks * strip
    me = lax.axis_index("chan")
    z, y, c = me // 4, (me // 2) % 2, me % 2

    def index(zz, yy, cc):
        return zz * 4 + yy * 2 + cc

    core_peer = index(z, y, 1 - c)
    y_peer = index(z, 1 - y, c)
    z_peers = [index((z + 1 + i) % 4, y, c) for i in range(3)]
    z_from = [index((z + 3 - i) % 4, y, c) for i in range(3)]
    right, left = (me + 1) % blocks, (me + blocks - 1) % blocks

    barrier = pltpu.get_barrier_semaphore()
    greeted = [core_peer, y_peer] + z_peers + ([left, right] if last else [])
    for peer in greeted:
        pl.semaphore_signal(barrier, inc=1, device_id={"chan": peer}, device_id_type=pl.DeviceIdType.MESH)

    def remote(src, dst, send, recv, peer):
        return pltpu.make_async_remote_copy(
            src_ref=src, dst_ref=dst, send_sem=send, recv_sem=recv,
            device_id={"chan": peer}, device_id_type=pl.DeviceIdType.MESH,
        )

    half_k = nrow // 2
    if not last:
        pl.semaphore_wait(barrier, len(greeted))
        other = pl.ds(pl.multiple_of((1 - c) * half_k, half_k), half_k)
        swap_d = remote(d_ref.at[:, :, other, :], got_d, half_s.at[0], half_r.at[0], core_peer)
        swap_h = remote(h_ref.at[:, other, :], got_h, half_s.at[1], half_r.at[1], core_peer)
        swap_d.start()
        swap_h.start()

    for t in range(sources):
        rows = s_ref[:, t].reshape(nrow, cols).astype(BF16)
        p = jnp.dot(rows, colcat_ref[...], preferred_element_type=F32)
        pst[0:nrow, t * cols : (t + 1) * cols] = p[:, :cols].astype(BF16)
        pst[nrow:, t * cols : (t + 1) * cols] = p[:, cols:].astype(BF16)

    tile = 128
    mine_k = pl.multiple_of(c * nrow, nrow)

    @pl.loop(0, nrow // tile)
    def _(kb):
        k0 = pl.multiple_of(kb * tile, tile)
        rows = fwd_ref[pl.ds(pl.multiple_of(mine_k + k0, tile), tile), :]
        qst[pl.ds(k0, tile), :] = jnp.dot(rows, pst[...], preferred_element_type=F32)

    if not last:
        swap_d.wait()
        swap_h.wait()
    thin = 16

    @pl.loop(0, half_k // thin)
    def _(kb):
        k0 = pl.multiple_of(kb * thin, thin)
        here = pl.ds(k0, thin)
        if last:
            h = [h_ref[p, here, :].astype(F32) for p in range(len(PAIRS))]
        else:
            whole = pl.ds(pl.multiple_of(c * half_k + k0, thin), thin)
            h = [(h_ref[p, whole, :].astype(F32) + got_h[p, here, :].astype(F32)) for p in range(len(PAIRS))]
            for p in range(len(PAIRS)):
                hsum_ref[p, here, :] = h[p].astype(BF16)
        for part in range(2):
            rows = pl.ds(pl.multiple_of(part * half_k + k0, thin), thin)
            q = [qst[rows, t * cols : (t + 1) * cols] for t in range(sources)]
            for s in range(sources):
                if last:
                    g = d_ref[part, s, here, :].astype(F32)
                else:
                    g = d_ref[part, s, whole, :].astype(F32) + got_d[part, s, here, :].astype(F32)
                    dsum_ref[part, s, here, :] = g.astype(BF16)
                for t in range(sources):
                    g = g - h[PAIR_OF[s, t]] * q[t]
                gst[rows, s * cols : (s + 1) * cols] = g.astype(BF16)

    if last:
        pl.semaphore_wait(barrier, len(greeted))

    core_copies, y_copies, z_copies = [], [], []

    def do_core(i):
        zb = (z + 1 + i) % 4
        r0 = pl.multiple_of(zb * tile, tile)
        r1 = pl.multiple_of(nrow + zb * tile, tile)
        ur = jnp.dot(bwd_ref[pl.ds(r0, tile), pl.ds(mine_k, nrow)], gst[...], preferred_element_type=F32).astype(BF16)
        ui = jnp.dot(bwd_ref[pl.ds(r1, tile), pl.ds(mine_k, nrow)], gst[...], preferred_element_type=F32).astype(BF16)
        for s in range(sources):
            both = jnp.concatenate([ur[:, s * cols : (s + 1) * cols], ui[:, s * cols : (s + 1) * cols]], axis=1)
            v = jnp.dot(both, colback_ref[...], preferred_element_type=F32)
            vb[i, :, :, s] = v.astype(BF16).reshape(2, 2, strip, cols)
        copy = remote(vb.at[i, :, 1 - c], got_core.at[i], core_s.at[i], core_r.at[i], core_peer)
        copy.start()
        core_copies.append(copy)

    def do_y(i):
        core_copies[i].wait()
        acc[i] = (vb[i, :, c].astype(F32) + got_core[i].astype(F32)).astype(BF16)
        copy = remote(acc.at[i, 1 - y], got_y.at[i], y_s.at[i], y_r.at[i], y_peer)
        copy.start()
        y_copies.append(copy)

    def do_z(i):
        y_copies[i].wait()
        fin[i] = (acc[i, y].astype(F32) + got_y[i].astype(F32)).astype(BF16)
        copy = remote(fin.at[i], got_z.at[i], z_s.at[i], z_r.at[i], z_peers[i])
        copy.start()
        z_copies.append(copy)

    do_core(0)
    do_core(1)
    do_y(0)
    do_core(2)
    do_y(1)
    do_z(0)
    do_core(3)
    do_y(2)
    do_z(1)
    do_y(3)
    do_z(2)
    y_copies[3].wait()
    total = acc[3, y].astype(F32) + got_y[3].astype(F32)
    for i in range(3):
        z_copies[i].wait()
        total = total + got_z[i].astype(F32)

    def bound(s, j):
        return lam_ref[s, j]

    if not last:
        vall[me] = total.astype(BF16)
        gz, gy, gc = [], [], []
        for i in range(3):
            copy = remote(vall.at[me], vall.at[me], gz_s.at[i], gz_r.at[i], z_peers[i])
            copy.start()
            gz.append(copy)

        def to_core(src, j):
            copy = remote(vall.at[src], vall.at[src], gc_s.at[j], gc_r.at[j], core_peer)
            copy.start()
            gc.append(copy)

        held = [me] + z_from
        for j in range(4):
            if j > 0:
                gz[j - 1].wait_recv()
            copy = remote(vall.at[held[j]], vall.at[held[j]], gy_s.at[j], gy_r.at[j], y_peer)
            copy.start()
            gy.append(copy)
            to_core(held[j], j)
        for j in range(4):
            gy[j].wait_recv()
            zz = (z + 4 - j) % 4
            to_core(index(zz, 1 - y, c), 4 + j)
        for copy in gc:
            copy.wait_recv()
        for copy in gz + gy + gc:
            copy.wait_send()
        xpad[:, 0:16] = jnp.zeros((sources, 16, cols), F32)
        xpad[:, nrow + 16 :] = jnp.zeros((sources, 16, cols), F32)

        @pl.loop(0, blocks)
        def _(b):
            xpad[:, pl.ds(pl.multiple_of(16 + b * strip, 16), strip)] = s_ref[b].astype(F32) + vall[b].astype(F32)

        xpad[:, pl.ds(pl.multiple_of(16 + me * strip, 16), strip)] = own_ref[...] + total

        @pl.loop(0, blocks)
        def _(b):
            start = pl.multiple_of(8 + b * strip, 8)
            for s in range(sources):
                x = xpad[s, pl.ds(start, strip + 16), :]
                out_ref[b, s] = smooth_window(x, b * strip - 8, nrow, bound(s, 0), bound(s, 1))
    else:
        mine = s_ref[me]
        vall[me] = total.astype(BF16)
        half = strip // 2
        to_right = remote(vall.at[me, :, half:strip], halo.at[0], halo_s.at[0], halo_r.at[0], right)
        to_left = remote(vall.at[me, :, 0:half], halo.at[1], halo_s.at[1], halo_r.at[1], left)
        to_right.start()
        to_left.start()
        xpad[:, 16 : 16 + strip] = mine + total
        above = s_ref[left, :, half:strip]
        below = s_ref[right, :, 0:half]
        to_right.wait()
        to_left.wait()
        above = above + halo[0].astype(F32)
        below = below + halo[1].astype(F32)
        xpad[:, 0:16] = jnp.where(me > 0, above, 0.0)
        xpad[:, 16 + strip : 32 + strip] = jnp.where(me < blocks - 1, below, 0.0)
        for s in range(sources):
            x = xpad[s, 8 : 24 + strip, :]
            out_ref[s] = smooth_window(x, me * strip - 8, nrow, bound(s, 0), bound(s, 1))


def step(last, s_full, own, dd, hh, tables, lam):
    blocks, sources, strip, cols = s_full.shape
    nrow = blocks * strip
    vm = pl.BlockSpec(memory_space=pltpu.VMEM)
    dma = pltpu.SemaphoreType.DMA
    block = (sources, strip, cols)
    sum_d = (2, sources, nrow // 2, cols)
    sum_h = (len(PAIRS), nrow // 2, cols)
    return pl.pallas_call(
        functools.partial(step_kernel, last),
        out_shape=jax.ShapeDtypeStruct(block, F32)
        if last
        else (
            jax.ShapeDtypeStruct((blocks,) + block, F32),
            jax.ShapeDtypeStruct(sum_d, BF16),
            jax.ShapeDtypeStruct(sum_h, BF16),
        ),
        in_specs=[vm] * 8 + [pl.BlockSpec(memory_space=pltpu.SMEM)],
        out_specs=vm if last else (vm, vm, vm),
        scratch_shapes=([] if last else [pltpu.VMEM(sum_d, BF16), pltpu.VMEM(sum_h, BF16)])
        + [
            pltpu.VMEM((nrow, sources * cols), F32),
            pltpu.VMEM((2 * nrow, sources * cols), BF16),
            pltpu.VMEM((nrow, sources * cols), BF16),
            pltpu.VMEM((4, 2, 2) + block, BF16),
            pltpu.VMEM((4, 2) + block, BF16),
            pltpu.VMEM((4, 2) + block, BF16),
            pltpu.VMEM((4,) + block, BF16),
            pltpu.VMEM((3,) + block, BF16),
            pltpu.VMEM((3,) + block, BF16),
            pltpu.VMEM((blocks,) + block, BF16),
            pltpu.VMEM((sources, (strip if last else nrow) + 32, cols), F32),
            pltpu.VMEM((2, sources, 16, cols), BF16),
            dma((4,)), dma((4,)), dma((4,)), dma((4,)), dma((3,)), dma((3,)),
            dma((3,)), dma((3,)), dma((4,)), dma((4,)), dma((8,)), dma((8,)),
            dma((2,)), dma((2,)), dma((2,)), dma((2,)),
        ],
        compiler_params=pltpu.CompilerParams(
            collective_id=1 if last else 0, has_side_effects=True, vmem_limit_bytes=VMEM_LIMIT
        ),
    )(s_full, own, dd, hh, *tables, lam)


def sums_kernel(d_ref, g_ref, mix_ref, level_ref, expand_ref, copy_d_ref, copy_h_ref, mask_d_ref, mask_h_ref,
                dd_ref, hh_ref, wd_ref, wh_ref):
    @pl.when(pl.program_id(0) == 0)
    def _():
        mix = mix_ref[...]
        weighted = mix * (level_ref[...].astype(F32) * 0.25)
        chans = mix.shape[1]
        by_source = [jnp.broadcast_to(weighted[s : s + 1], (16, chans)) for s in range(4)]
        by_pair = [jnp.broadcast_to(weighted[s : s + 1] * mix[t : t + 1], (8, chans)) for s, t in PAIRS]
        wd = jnp.concatenate(by_source + by_source, axis=0).astype(BF16)
        wh = jnp.concatenate(by_pair, axis=0).astype(BF16)
        wd = jnp.dot(wd, copy_d_ref[...], preferred_element_type=F32) * mask_d_ref[...].astype(F32)
        wh = jnp.dot(wh, copy_h_ref[...], preferred_element_type=F32) * mask_h_ref[...].astype(F32)
        wd_ref[...] = wd.astype(BF16)
        wh_ref[...] = wh.astype(BF16)

    groups = g_ref.shape[0] // 8
    chans, cols = g_ref.shape[1:]
    wide = 4 * chans
    half = cols // 2
    for n in range(groups):
        g = g_ref[8 * n : 8 * n + 8]
        products = []
        for j in range(0, 8, 2):
            pair = [jnp.concatenate([g[k, :, :half], g[k, :, half:]], axis=0) for k in (j, j + 1)]
            spread = jnp.dot(expand_ref[...], jnp.concatenate(pair, axis=1), preferred_element_type=F32)
            for i in range(2):
                row = (8 * n + j + i) * wide
                d = d_ref[row : row + wide, :].astype(F32)
                products.append((d * spread[:, i * half : (i + 1) * half]).astype(BF16))
        total = jnp.dot(wd_ref[...], jnp.concatenate(products, axis=0), preferred_element_type=F32)
        for z in range(2):
            for s in range(4):
                for lt in range(2):
                    r = ((z * 4 + s) * 2 + lt) * 8
                    dd_ref[z, s, 8 * n : 8 * n + 8, lt * half : (lt + 1) * half] = total[r : r + 8].astype(BF16)
        squares = g.astype(F32)
        squares = (squares * squares).astype(BF16).reshape(8 * chans, cols)
        grams = jnp.dot(wh_ref[...], squares, preferred_element_type=F32)
        for p in range(len(PAIRS)):
            hh_ref[p, 8 * n : 8 * n + 8, :] = grams[8 * p : 8 * p + 8].astype(BF16)


def channel_sums(sky_data, beam_gains, mixing, noise_levels):
    nrow, chans, _, cols = sky_data.shape
    half = cols // 2
    ones = np.ones
    eye = np.eye
    mask_d = np.einsum("s,kK,lL,zZ,c->zslkKcLZ", ones(4), eye(8), eye(2), eye(2), ones(chans)).reshape(128, -1)
    mask_h = np.einsum("p,kK,c->pkKc", ones(len(PAIRS)), eye(8), ones(chans)).reshape(8 * len(PAIRS), -1)
    copy_d = np.einsum("cC,k,r->ckCr", eye(chans), ones(8), ones(4)).reshape(chans, -1)
    copy_h = np.einsum("cC,k->ckC", eye(chans), ones(8)).reshape(chans, -1)
    expand = np.einsum("cC,lL,z->clzLC", np.eye(chans), np.eye(2), np.ones(2)).reshape(4 * chans, 2 * chans)
    rows = jnp.swapaxes(sky_data.reshape(nrow, chans, 2, 2, half), 2, 3).reshape(-1, half)
    tile = 32
    tables = [jnp.asarray(t.astype(ml_dtypes.bfloat16)) for t in (expand, copy_d, copy_h, mask_d, mask_h)]
    return pl.pallas_call(
        sums_kernel,
        grid=(nrow // tile,),
        out_shape=(
            jax.ShapeDtypeStruct((2, 4, nrow, cols), BF16),
            jax.ShapeDtypeStruct((len(PAIRS), nrow, cols), BF16),
        ),
        in_specs=[
            pl.BlockSpec((tile * 4 * chans, half), lambda i: (i, 0)),
            pl.BlockSpec((tile, chans, cols), lambda i: (i, 0, 0)),
            pl.BlockSpec((4, chans), lambda i: (0, 0)),
            pl.BlockSpec((1, chans), lambda i: (0, 0)),
        ]
        + [pl.BlockSpec(table.shape, lambda i: (0, 0)) for table in tables],
        out_specs=(
            pl.BlockSpec((2, 4, tile, cols), lambda i: (0, 0, i, 0)),
            pl.BlockSpec((len(PAIRS), tile, cols), lambda i: (0, i, 0)),
        ),
        scratch_shapes=[pltpu.VMEM((128, 32 * chans), BF16), pltpu.VMEM((8 * len(PAIRS), 8 * chans), BF16)],
        compiler_params=pltpu.CompilerParams(vmem_limit_bytes=VMEM_LIMIT),
        cost_estimate=pl.CostEstimate(flops=2 * 10**9, bytes_accessed=30 * 10**6, transcendentals=0),
    )(rows, beam_gains, mixing.T, noise_levels.reshape(1, chans), *tables)


def body(sky_data, beam_gains, mixing, noise_levels, threshold_levels, start_sources):
    strip, sources, cols = start_sources.shape
    blocks = lax.axis_size("chan")
    if blocks != 16 or strip != 32 or sources != 4 or cols != 256 or sky_data.shape[1] != 32:
        return plain_body(sky_data, beam_gains, mixing, noise_levels, threshold_levels, start_sources)
    row_real, row_imag = host_tables(strip * blocks)
    col_real, col_imag = host_tables(cols)
    forward = np.block([[row_real, -row_imag], [row_imag, row_real]])
    backward = np.block([[row_real, row_imag], [-row_imag, row_real]])
    half_k = strip * blocks // 2
    starts = [0, 2 * half_k, half_k, 3 * half_k]
    tables = [
        jnp.asarray(np.concatenate([col_real, col_imag], axis=1)),
        jnp.asarray(np.concatenate([col_real, col_imag], axis=0)),
        jnp.asarray(np.concatenate([forward[part : part + half_k] for part in starts], axis=0)),
        jnp.asarray(np.concatenate([backward[:, part : part + half_k] for part in starts], axis=1)),
    ]
    lam = threshold_levels.astype(F32) * 0.05
    own = jnp.swapaxes(start_sources, 0, 1)
    s_full = lax.all_gather(own.astype(BF16), "chan", axis=0)
    dd, hh = channel_sums(sky_data, beam_gains, mixing, noise_levels)
    s_full, dd, hh = step(False, s_full, own, dd, hh, tables, lam)
    result = step(True, s_full, own, dd, hh, tables, lam)
    return jnp.swapaxes(result, 0, 1)


def solution(mesh):
    return jax.shard_map(
        body,
        mesh=mesh,
        in_specs=(
            P("groups", "chan", None, None),
            P("groups", "chan", None),
            P(("groups", "chan"), None),
            P("chan"),
            P(),
            P(("groups", "chan"), None, None),
        ),
        out_specs=P(("groups", "chan"), None, None),
        check_vma=False,
    )
```

```python
import functools
import math

import jax
import jax.numpy as jnp
import ml_dtypes
import numpy as np
from jax import lax
from jax.experimental import pallas as pl
from jax.experimental.pallas import tpu as pltpu
from jax.sharding import PartitionSpec as P

ITERS = 2


def padded_2(cells, sides, width):
    for axis, dim in sides:
        count = lax.axis_size(axis)
        ends = count - 1
        head = lax.slice_in_dim(cells, 0, width, axis=dim)
        tail = lax.slice_in_dim(cells, cells.shape[dim] - width, cells.shape[dim], axis=dim)
        cells = jnp.concatenate(
            [
                lax.ppermute(tail, axis, [(i, (i + 1) % count) for i in range(ends)]),
                cells,
                lax.ppermute(head, axis, [((i + 1) % count, i) for i in range(ends)]),
            ],
            axis=dim,
        )
    return cells


def dft_tables(length):
    positions = jnp.arange(length, dtype=jnp.int32)
    angles = (positions[:, None] * positions[None, :] % length).astype(jnp.float32) * (
        2.0 * math.pi / length
    )
    norm_factor = 1.0 / math.sqrt(length)
    return (
        (jnp.cos(angles) * norm_factor).astype(jnp.bfloat16),
        (-jnp.sin(angles) * norm_factor).astype(jnp.bfloat16),
    )


def column_part(rounded, col_cat):
    row_count, source_count, col_count = rounded.shape
    product = jnp.dot(
        rounded.reshape(row_count * source_count, col_count),
        col_cat,
        preferred_element_type=jnp.float32,
    )
    return product.astype(jnp.bfloat16).reshape(row_count, source_count * 2 * col_count)


def combine_forward(real_prod, imag_prod, source_count, col_count):
    real_prod = real_prod.reshape(real_prod.shape[0], source_count, 2, col_count)
    imag_prod = imag_prod.reshape(imag_prod.shape[0], source_count, 2, col_count)
    real_out = real_prod[:, :, 0] - imag_prod[:, :, 1]
    imag_out = real_prod[:, :, 1] + imag_prod[:, :, 0]
    return jnp.stack([real_out, imag_out], axis=2)


def inverse_rows(row_real, row_imag, packed_grad, col_back, source_count, col_count):
    real_prod = jnp.dot(row_real, packed_grad, preferred_element_type=jnp.float32)
    imag_prod = jnp.dot(row_imag, packed_grad, preferred_element_type=jnp.float32)
    real_prod = real_prod.reshape(real_prod.shape[0], source_count, 2, col_count)
    imag_prod = imag_prod.reshape(imag_prod.shape[0], source_count, 2, col_count)
    real_out = real_prod[:, :, 0] + imag_prod[:, :, 1]
    imag_out = real_prod[:, :, 1] - imag_prod[:, :, 0]
    joined = jnp.concatenate([real_out, imag_out], axis=-1).astype(jnp.bfloat16)
    result = jnp.dot(
        joined.reshape(-1, 2 * col_count), col_back, preferred_element_type=jnp.float32
    )
    return result.reshape(real_prod.shape[0], source_count, col_count)


def block_gradient(fourier, data_block, beam_block, mix_block, level_block):
    predicted = jnp.einsum("ct,ktzl->kczl", mix_block, fourier)
    beam_gain = beam_block.astype(jnp.float32)[:, :, None, :]
    residual = data_block.astype(jnp.float32) - beam_gain * predicted
    weight = level_block.astype(jnp.float32) * 0.25
    weighted = weight[None, :, None, None] * beam_gain * residual
    summed = jnp.einsum("cs,kczl->kszl", mix_block, weighted)
    return summed.astype(jnp.bfloat16)


def smooth_rows(padded, spacing, row_count):
    return (
        padded[0:row_count]
        + 2.0 * padded[spacing : spacing + row_count]
        + padded[2 * spacing : 2 * spacing + row_count]
    ) * 0.25


def smooth_cols(values, spacing):
    padded = jnp.pad(values, ((0, 0), (0, 0), (spacing, spacing)))
    return (
        padded[..., : -2 * spacing]
        + 2.0 * padded[..., spacing:-spacing]
        + padded[..., 2 * spacing :]
    ) * 0.25


def shrink(values, bound_value):
    return values - jnp.clip(values, -bound_value, bound_value)


def combine_scales(updated, smooth_one, coarse, fine_bound, coarse_bound):
    return (
        coarse
        + shrink(smooth_one - coarse, coarse_bound)
        + shrink(updated - smooth_one, fine_bound)
    )


def plain_body(sky_data, beam_gains, mixing, noise_levels, threshold_levels, start_sources):
    strip_rows, source_count, col_count = start_sources.shape
    full_rows = strip_rows * lax.axis_size("chan")
    row_real, row_imag = dft_tables(full_rows)
    col_real, col_imag = dft_tables(col_count)
    col_cat = jnp.concatenate([col_real, col_imag], axis=1)
    col_back = jnp.concatenate([col_real, col_imag], axis=0)
    bounds = threshold_levels.astype(jnp.float32) * 0.05
    fine_bound = bounds[:, 0][:, None]
    coarse_bound = bounds[:, 1][:, None]
    sources = start_sources
    for iteration in range(ITERS):
        rounded = sources.astype(jnp.bfloat16)
        gathered = lax.all_gather(rounded, "chan", axis=0, tiled=True)
        packed = column_part(gathered, col_cat)
        fourier = combine_forward(
            jnp.dot(row_real, packed, preferred_element_type=jnp.float32),
            jnp.dot(row_imag, packed, preferred_element_type=jnp.float32),
            source_count,
            col_count,
        )
        grad_local = block_gradient(fourier, sky_data, beam_gains, mixing, noise_levels)
        packed_grad = grad_local.reshape(full_rows, source_count * 2 * col_count)
        gradient = lax.psum_scatter(
            inverse_rows(row_real, row_imag, packed_grad, col_back, source_count, col_count),
            "chan",
            scatter_dimension=0,
            tiled=True,
        )
        updated = sources + gradient
        fine_pad = padded_2(updated, (("chan", 0),), 1)
        smooth_one = smooth_cols(smooth_rows(fine_pad, 1, strip_rows), 1)
        coarse_pad = padded_2(smooth_one, (("chan", 0),), 2)
        coarse = smooth_cols(smooth_rows(coarse_pad, 2, strip_rows), 2)
        sources = combine_scales(updated, smooth_one, coarse, fine_bound, coarse_bound)
    return sources


BF16 = jnp.bfloat16
F32 = jnp.float32
VMEM_LIMIT = 56 * 1024 * 1024
PAIRS = [(s, t) for s in range(4) for t in range(s, 4)]
PAIR_OF = {}
for number, (first, second) in enumerate(PAIRS):
    PAIR_OF[first, second] = number
    PAIR_OF[second, first] = number


def host_tables(length):
    positions = np.arange(length)
    angles = (positions[:, None] * positions[None, :] % length) * (2.0 * math.pi / length)
    norm_factor = 1.0 / math.sqrt(length)
    return (
        (np.cos(angles) * norm_factor).astype(np.float32).astype(ml_dtypes.bfloat16),
        (-np.sin(angles) * norm_factor).astype(np.float32).astype(ml_dtypes.bfloat16),
    )


def smooth_window(x, first_row, row_total, fine, coarse_bound):
    height, width = x.shape
    rows = lax.broadcasted_iota(jnp.int32, (height, width), 0) + first_row
    lanes = lax.broadcasted_iota(jnp.int32, (height, width), 1)
    inside = (rows >= 0) & (rows < row_total)

    def smooth(v, d):
        v = 0.25 * (pltpu.roll(v, d, 0) + 2.0 * v + pltpu.roll(v, height - d, 0))
        left = jnp.where(lanes >= d, pltpu.roll(v, d, 1), 0.0)
        right = jnp.where(lanes < width - d, pltpu.roll(v, width - d, 1), 0.0)
        return 0.25 * (left + 2.0 * v + right)

    c1 = jnp.where(inside, smooth(x, 1), 0.0)
    c2 = smooth(c1, 2)
    d1 = c1 - c2
    d0 = x - c1
    result = c2 + (d1 - jnp.clip(d1, -coarse_bound, coarse_bound)) + (d0 - jnp.clip(d0, -fine, fine))
    return result[8 : height - 8]


class Place:
    def __init__(self):
        self.me = me = lax.axis_index("chan")
        self.z, self.y, self.c = z, y, c = me // 4, (me // 2) % 2, me % 2
        self.core_peer = self.index(z, y, 1 - c)
        self.y_peer = self.index(z, 1 - y, c)
        self.z_peers = [self.index((z + 1 + i) % 4, y, c) for i in range(3)]
        self.peers = [self.core_peer, self.y_peer] + self.z_peers

    def index(self, z, y, c):
        return z * 4 + y * 2 + c

    def remote(self, src, dst, send, recv, peer):
        return pltpu.make_async_remote_copy(
            src_ref=src, dst_ref=dst, send_sem=send, recv_sem=recv,
            device_id={"chan": peer}, device_id_type=pl.DeviceIdType.MESH,
        )

    def greet(self, peers):
        barrier = pltpu.get_barrier_semaphore()
        for peer in peers:
            pl.semaphore_signal(barrier, inc=1, device_id={"chan": peer}, device_id_type=pl.DeviceIdType.MESH)

    def gather(self, buf, gz_s, gz_r, gy_s, gy_r, gc_s, gc_r):
        z, y, c = self.z, self.y, self.c
        held = [self.index((z + 4 - j) % 4, y, c) for j in range(4)]
        crossed = [self.index((z + 4 - j) % 4, 1 - y, c) for j in range(4)]

        def send(block, s_sem, r_sem, peer):
            return self.remote(buf.at[block], buf.at[block], s_sem, r_sem, peer)

        gz = [send(held[0], gz_s.at[i], gz_r.at[i], self.z_peers[i]) for i in range(3)]
        gy = [send(held[j], gy_s.at[j], gy_r.at[j], self.y_peer) for j in range(4)]
        gc = [send(block, gc_s.at[j], gc_r.at[j], self.core_peer) for j, block in enumerate(held + crossed)]
        return gz, gy, gc


def steps_kernel(
    s_ref, start_ref, d_ref, h_ref, colcat_ref, colback_ref, fwd_ref, bwd_ref, lam_ref, out_ref,
    got_d, got_h, dsum_ref, hsum_ref, qst, pst, gst, vb, got_core, acc, got_y, fin, got_z, sall, own, xpad, halo,
    core_s, core_r, y_s, y_r, z_s, z_r, gz_s, gz_r, gy_s, gy_r, gc_s, gc_r, halo_s, halo_r, half_s, half_r,
):
    blocks, sources, strip, cols = s_ref.shape
    nrow = blocks * strip
    place = Place()
    me, z, y, c = place.me, place.z, place.y, place.c
    remote = place.remote
    right, left = (me + 1) % blocks, (me + blocks - 1) % blocks
    greeted = place.peers + [left, right]
    place.greet(greeted)
    pl.semaphore_wait(pltpu.get_barrier_semaphore(), len(greeted))

    half_k = nrow // 2
    other = pl.ds(pl.multiple_of((1 - c) * half_k, half_k), half_k)
    swap_d = remote(d_ref.at[:, :, other, :], got_d, half_s.at[0], half_r.at[0], place.core_peer)
    swap_h = remote(h_ref.at[:, other, :], got_h, half_s.at[1], half_r.at[1], place.core_peer)
    swap_d.start()
    swap_h.start()
    for s in range(sources):
        own[s] = start_ref[:, s, :]

    tile = 128
    thin = 16
    mine_k = pl.multiple_of(c * nrow, nrow)
    for iteration in range(ITERS):
        first, last = iteration == 0, iteration == ITERS - 1
        now_ref = s_ref if first else sall

        for t in range(sources):
            p = jnp.dot(now_ref[:, t].reshape(nrow, cols), colcat_ref[...], preferred_element_type=F32)
            pst[0:nrow, t * cols : (t + 1) * cols] = p[:, :cols].astype(BF16)
            pst[nrow:, t * cols : (t + 1) * cols] = p[:, cols:].astype(BF16)

        @pl.loop(0, nrow // tile)
        def _(kb):
            k0 = pl.multiple_of(kb * tile, tile)
            rows = fwd_ref[pl.ds(pl.multiple_of(mine_k + k0, tile), tile), :]
            qst[pl.ds(k0, tile), :] = jnp.dot(rows, pst[...], preferred_element_type=F32)

        if first:
            swap_d.wait()
            swap_h.wait()

        @pl.loop(0, half_k // thin)
        def _(kb):
            k0 = pl.multiple_of(kb * thin, thin)
            here = pl.ds(k0, thin)
            if first:
                whole = pl.ds(pl.multiple_of(c * half_k + k0, thin), thin)
                h = [(h_ref[p, whole, :].astype(F32) + got_h[p, here, :].astype(F32)) for p in range(len(PAIRS))]
                for p in range(len(PAIRS)):
                    hsum_ref[p, here, :] = h[p].astype(BF16)
            else:
                h = [hsum_ref[p, here, :].astype(F32) for p in range(len(PAIRS))]
            for part in range(2):
                rows = pl.ds(pl.multiple_of(part * half_k + k0, thin), thin)
                q = [qst[rows, t * cols : (t + 1) * cols] for t in range(sources)]
                for s in range(sources):
                    if first:
                        g = d_ref[part, s, whole, :].astype(F32) + got_d[part, s, here, :].astype(F32)
                        dsum_ref[part, s, here, :] = g.astype(BF16)
                    else:
                        g = dsum_ref[part, s, here, :].astype(F32)
                    for t in range(sources):
                        g = g - h[PAIR_OF[s, t]] * q[t]
                    gst[rows, s * cols : (s + 1) * cols] = g.astype(BF16)

        core_copies, y_copies, z_copies = [], [], []

        def do_core(i):
            zb = (z + 1 + i) % 4
            r0 = pl.multiple_of(zb * tile, tile)
            r1 = pl.multiple_of(nrow + zb * tile, tile)
            columns = pl.ds(mine_k, nrow)
            ur = jnp.dot(bwd_ref[pl.ds(r0, tile), columns], gst[...], preferred_element_type=F32).astype(BF16)
            ui = jnp.dot(bwd_ref[pl.ds(r1, tile), columns], gst[...], preferred_element_type=F32).astype(BF16)
            for s in range(sources):
                both = jnp.concatenate([ur[:, s * cols : (s + 1) * cols], ui[:, s * cols : (s + 1) * cols]], axis=1)
                v = jnp.dot(both, colback_ref[...], preferred_element_type=F32)
                vb[i, :, :, s] = v.astype(BF16).reshape(2, 2, strip, cols)
            copy = remote(vb.at[i, :, 1 - c], got_core.at[i], core_s.at[i], core_r.at[i], place.core_peer)
            copy.start()
            core_copies.append(copy)

        def do_y(i):
            core_copies[i].wait()
            acc[i] = (vb[i, :, c].astype(F32) + got_core[i].astype(F32)).astype(BF16)
            copy = remote(acc.at[i, 1 - y], got_y.at[i], y_s.at[i], y_r.at[i], place.y_peer)
            copy.start()
            y_copies.append(copy)

        def do_z(i):
            y_copies[i].wait()
            fin[i] = (acc[i, y].astype(F32) + got_y[i].astype(F32)).astype(BF16)
            copy = remote(fin.at[i], got_z.at[i], z_s.at[i], z_r.at[i], place.z_peers[i])
            copy.start()
            z_copies.append(copy)

        do_core(0)
        do_core(1)
        do_y(0)
        do_core(2)
        do_y(1)
        do_z(0)
        do_core(3)
        do_y(2)
        do_z(1)
        do_y(3)
        do_z(2)
        y_copies[3].wait()
        total = own[...] + (acc[3, y].astype(F32) + got_y[3].astype(F32))
        for i in range(3):
            z_copies[i].wait()
            total = total + got_z[i].astype(F32)

        xpad[:, 8 : 8 + strip] = total
        to_right = remote(xpad.at[:, strip : strip + 8], halo.at[0], halo_s.at[0], halo_r.at[0], right)
        to_left = remote(xpad.at[:, 8:16], halo.at[1], halo_s.at[1], halo_r.at[1], left)
        to_right.start()
        to_left.start()
        to_right.wait()
        to_left.wait()
        xpad[:, 0:8] = jnp.where(me > 0, halo[0], 0.0)
        xpad[:, 8 + strip : 16 + strip] = jnp.where(me < blocks - 1, halo[1], 0.0)
        for s in range(sources):
            result = smooth_window(xpad[s], me * strip - 8, nrow, lam_ref[s, 0], lam_ref[s, 1])
            if last:
                out_ref[:, s, :] = result
            else:
                own[s] = result
                sall[me, s] = result.astype(BF16)

        if not last:
            gz, gy, gc = place.gather(sall, gz_s, gz_r, gy_s, gy_r, gc_s, gc_r)
            for copy in gz + [gy[0], gc[0]]:
                copy.start()
            for j in range(1, 4):
                gz[j - 1].wait_recv()
                gy[j].start()
                gc[j].start()
            for j in range(4):
                gy[j].wait_recv()
                gc[4 + j].start()
            for copy in gc:
                copy.wait_recv()
            for copy in gz + gy + gc:
                copy.wait_send()


def steps(s_full, start, dd, hh, tables, lam):
    blocks, sources, strip, cols = s_full.shape
    nrow = blocks * strip
    vm = pl.BlockSpec(memory_space=pltpu.VMEM)
    dma = pltpu.SemaphoreType.DMA
    block = (sources, strip, cols)
    sum_d = (2, sources, nrow // 2, cols)
    sum_h = (len(PAIRS), nrow // 2, cols)
    return pl.pallas_call(
        steps_kernel,
        out_shape=jax.ShapeDtypeStruct(start.shape, F32),
        in_specs=[vm] * 8 + [pl.BlockSpec(memory_space=pltpu.SMEM)],
        out_specs=vm,
        scratch_shapes=[
            pltpu.VMEM(sum_d, BF16),
            pltpu.VMEM(sum_h, BF16),
            pltpu.VMEM(sum_d, BF16),
            pltpu.VMEM(sum_h, BF16),
            pltpu.VMEM((nrow, sources * cols), F32),
            pltpu.VMEM((2 * nrow, sources * cols), BF16),
            pltpu.VMEM((nrow, sources * cols), BF16),
            pltpu.VMEM((4, 2, 2) + block, BF16),
            pltpu.VMEM((4, 2) + block, BF16),
            pltpu.VMEM((4, 2) + block, BF16),
            pltpu.VMEM((4,) + block, BF16),
            pltpu.VMEM((3,) + block, BF16),
            pltpu.VMEM((3,) + block, BF16),
            pltpu.VMEM((blocks,) + block, BF16),
            pltpu.VMEM(block, F32),
            pltpu.VMEM((sources, strip + 16, cols), F32),
            pltpu.VMEM((2, sources, 8, cols), F32),
            dma((4,)), dma((4,)), dma((4,)), dma((4,)), dma((3,)), dma((3,)),
            dma((3,)), dma((3,)), dma((4,)), dma((4,)), dma((8,)), dma((8,)),
            dma((2,)), dma((2,)), dma((2,)), dma((2,)),
        ],
        compiler_params=pltpu.CompilerParams(collective_id=0, has_side_effects=True, vmem_limit_bytes=VMEM_LIMIT),
    )(s_full, start, dd, hh, *tables, lam)


def sums_kernel(start_ref, d_ref, g_ref, mix_ref, level_ref, expand_ref, copy_d_ref, copy_h_ref, mask_d_ref, mask_h_ref,
                dd_ref, hh_ref, s_ref, wd_ref, wh_ref, own, own_sem, *gather_sems):
    at = pl.program_id(0)
    place = Place()
    gz, gy, gc = place.gather(s_ref, *gather_sems)
    keep = pltpu.make_async_copy(own, s_ref.at[place.me], own_sem)

    @pl.when(at == 0)
    def _():
        place.greet(place.peers)
        for s in range(4):
            own[s] = start_ref[:, s, :].astype(BF16)
        keep.start()

    @pl.when(at == 1)
    def _():
        keep.wait()
        pl.semaphore_wait(pltpu.get_barrier_semaphore(), len(place.peers))
        for copy in gz + [gy[0], gc[0]]:
            copy.start()

    @pl.when(at == 5)
    def _():
        for j in range(1, 4):
            gz[j - 1].wait_recv()
            gy[j].start()
            gc[j].start()

    @pl.when(at == 9)
    def _():
        for j in range(4):
            gy[j].wait_recv()
            gc[4 + j].start()

    @pl.when(at == pl.num_programs(0) - 1)
    def _():
        for copy in gc:
            copy.wait_recv()
        for copy in gz + gy + gc:
            copy.wait_send()

    @pl.when(pl.program_id(0) == 0)
    def _():
        mix = mix_ref[...]
        weighted = mix * (level_ref[...].astype(F32) * 0.25)
        chans = mix.shape[1]
        by_source = [jnp.broadcast_to(weighted[s : s + 1], (16, chans)) for s in range(4)]
        by_pair = [jnp.broadcast_to(weighted[s : s + 1] * mix[t : t + 1], (8, chans)) for s, t in PAIRS]
        wd = jnp.concatenate(by_source + by_source, axis=0).astype(BF16)
        wh = jnp.concatenate(by_pair, axis=0).astype(BF16)
        wd = jnp.dot(wd, copy_d_ref[...], preferred_element_type=F32) * mask_d_ref[...].astype(F32)
        wh = jnp.dot(wh, copy_h_ref[...], preferred_element_type=F32) * mask_h_ref[...].astype(F32)
        wd_ref[...] = wd.astype(BF16)
        wh_ref[...] = wh.astype(BF16)

    groups = g_ref.shape[0] // 16
    chans, cols = g_ref.shape[1:]
    wide = 4 * chans
    half = cols // 2
    for n in range(groups):
        products = []
        for j in range(8):
            ks = (16 * n + j, 16 * n + 8 + j)
            pair = [jnp.concatenate([g_ref[k, :, :half], g_ref[k, :, half:]], axis=0) for k in ks]
            spread = jnp.dot(expand_ref[...], jnp.concatenate(pair, axis=1), preferred_element_type=F32)
            d = jnp.concatenate([d_ref[k * wide : (k + 1) * wide, :] for k in ks], axis=1)
            products.append((d.astype(F32) * spread).astype(BF16))
        total = jnp.dot(wd_ref[...], jnp.concatenate(products, axis=0), preferred_element_type=F32)
        for r in range(16):
            z, s, lt = r // 8, r // 2 % 4, r % 2
            rows = total[8 * r : 8 * r + 8]
            both = jnp.concatenate([rows[:, :half], rows[:, half:]], axis=0)
            dd_ref[z, s, 16 * n : 16 * n + 16, lt * half : (lt + 1) * half] = both.astype(BF16)
        grams = []
        for k in (16 * n, 16 * n + 8):
            squares = g_ref[k : k + 8].astype(F32)
            squares = (squares * squares).astype(BF16).reshape(8 * chans, cols)
            grams.append(jnp.dot(wh_ref[...], squares, preferred_element_type=F32))
        for p in range(len(PAIRS)):
            both = jnp.concatenate([gram[8 * p : 8 * p + 8] for gram in grams], axis=0)
            hh_ref[p, 16 * n : 16 * n + 16, :] = both.astype(BF16)


def channel_sums(sky_data, beam_gains, mixing, noise_levels, start):
    nrow, chans, _, cols = sky_data.shape
    strip, sources, _ = start.shape
    blocks = nrow // strip
    dma = pltpu.SemaphoreType.DMA
    half = cols // 2
    ones = np.ones
    eye = np.eye
    mask_d = np.einsum("s,kK,lL,zZ,c->zslkKcLZ", ones(4), eye(8), eye(2), eye(2), ones(chans)).reshape(128, -1)
    mask_h = np.einsum("p,kK,c->pkKc", ones(len(PAIRS)), eye(8), ones(chans)).reshape(8 * len(PAIRS), -1)
    copy_d = np.einsum("cC,k,r->ckCr", eye(chans), ones(8), ones(4)).reshape(chans, -1)
    copy_h = np.einsum("cC,k->ckC", eye(chans), ones(8)).reshape(chans, -1)
    expand = np.einsum("cC,lL,z->clzLC", np.eye(chans), np.eye(2), np.ones(2)).reshape(4 * chans, 2 * chans)
    rows = jnp.swapaxes(sky_data.reshape(nrow, chans, 2, 2, half), 2, 3).reshape(-1, half)
    tile = 32
    tables = [jnp.asarray(t.astype(ml_dtypes.bfloat16)) for t in (expand, copy_d, copy_h, mask_d, mask_h)]
    return pl.pallas_call(
        sums_kernel,
        grid=(nrow // tile,),
        out_shape=(
            jax.ShapeDtypeStruct((2, 4, nrow, cols), BF16),
            jax.ShapeDtypeStruct((len(PAIRS), nrow, cols), BF16),
            jax.ShapeDtypeStruct((blocks, sources, strip, cols), BF16),
        ),
        in_specs=[
            pl.BlockSpec(start.shape, lambda i: (0, 0, 0)),
            pl.BlockSpec((tile * 4 * chans, half), lambda i: (i, 0)),
            pl.BlockSpec((tile, chans, cols), lambda i: (i, 0, 0)),
            pl.BlockSpec((4, chans), lambda i: (0, 0)),
            pl.BlockSpec((1, chans), lambda i: (0, 0)),
        ]
        + [pl.BlockSpec(table.shape, lambda i: (0, 0)) for table in tables],
        out_specs=(
            pl.BlockSpec((2, 4, tile, cols), lambda i: (0, 0, i, 0)),
            pl.BlockSpec((len(PAIRS), tile, cols), lambda i: (0, i, 0)),
            pl.BlockSpec(memory_space=pl.ANY),
        ),
        scratch_shapes=[
            pltpu.VMEM((128, 32 * chans), BF16),
            pltpu.VMEM((8 * len(PAIRS), 8 * chans), BF16),
            pltpu.VMEM((sources, strip, cols), BF16),
            dma, dma((3,)), dma((3,)), dma((4,)), dma((4,)), dma((8,)), dma((8,)),
        ],
        compiler_params=pltpu.CompilerParams(collective_id=1, has_side_effects=True, vmem_limit_bytes=VMEM_LIMIT),
        cost_estimate=pl.CostEstimate(flops=2 * 10**9, bytes_accessed=30 * 10**6, transcendentals=0),
    )(start, rows, beam_gains, mixing.T, noise_levels.reshape(1, chans), *tables)


def body(sky_data, beam_gains, mixing, noise_levels, threshold_levels, start_sources):
    strip, sources, cols = start_sources.shape
    blocks = lax.axis_size("chan")
    if blocks != 16 or strip != 32 or sources != 4 or cols != 256 or sky_data.shape[1] != 32:
        return plain_body(sky_data, beam_gains, mixing, noise_levels, threshold_levels, start_sources)
    row_real, row_imag = host_tables(strip * blocks)
    col_real, col_imag = host_tables(cols)
    forward = np.block([[row_real, -row_imag], [row_imag, row_real]])
    backward = np.block([[row_real, row_imag], [-row_imag, row_real]])
    half_k = strip * blocks // 2
    starts = [0, 2 * half_k, half_k, 3 * half_k]
    tables = [
        jnp.asarray(np.concatenate([col_real, col_imag], axis=1)),
        jnp.asarray(np.concatenate([col_real, col_imag], axis=0)),
        jnp.asarray(np.concatenate([forward[part : part + half_k] for part in starts], axis=0)),
        jnp.asarray(np.concatenate([backward[:, part : part + half_k] for part in starts], axis=1)),
    ]
    lam = threshold_levels.astype(F32) * 0.05
    dd, hh, s_full = channel_sums(sky_data, beam_gains, mixing, noise_levels, start_sources)
    return steps(s_full, start_sources, dd, hh, tables, lam)


def solution(mesh):
    return jax.shard_map(
        body,
        mesh=mesh,
        in_specs=(
            P("groups", "chan", None, None),
            P("groups", "chan", None),
            P(("groups", "chan"), None),
            P("chan"),
            P(),
            P(("groups", "chan"), None, None),
        ),
        out_specs=P(("groups", "chan"), None, None),
        check_vma=False,
    )
```

```python
import functools
import math

import jax
import jax.numpy as jnp
import ml_dtypes
import numpy as np
from jax import lax
from jax.experimental import pallas as pl
from jax.experimental.pallas import tpu as pltpu
from jax.sharding import PartitionSpec as P

ITERS = 2


def padded_2(cells, sides, width):
    for axis, dim in sides:
        count = lax.axis_size(axis)
        ends = count - 1
        head = lax.slice_in_dim(cells, 0, width, axis=dim)
        tail = lax.slice_in_dim(cells, cells.shape[dim] - width, cells.shape[dim], axis=dim)
        cells = jnp.concatenate(
            [
                lax.ppermute(tail, axis, [(i, (i + 1) % count) for i in range(ends)]),
                cells,
                lax.ppermute(head, axis, [((i + 1) % count, i) for i in range(ends)]),
            ],
            axis=dim,
        )
    return cells


def dft_tables(length):
    positions = jnp.arange(length, dtype=jnp.int32)
    angles = (positions[:, None] * positions[None, :] % length).astype(jnp.float32) * (
        2.0 * math.pi / length
    )
    norm_factor = 1.0 / math.sqrt(length)
    return (
        (jnp.cos(angles) * norm_factor).astype(jnp.bfloat16),
        (-jnp.sin(angles) * norm_factor).astype(jnp.bfloat16),
    )


def column_part(rounded, col_cat):
    row_count, source_count, col_count = rounded.shape
    product = jnp.dot(
        rounded.reshape(row_count * source_count, col_count),
        col_cat,
        preferred_element_type=jnp.float32,
    )
    return product.astype(jnp.bfloat16).reshape(row_count, source_count * 2 * col_count)


def combine_forward(real_prod, imag_prod, source_count, col_count):
    real_prod = real_prod.reshape(real_prod.shape[0], source_count, 2, col_count)
    imag_prod = imag_prod.reshape(imag_prod.shape[0], source_count, 2, col_count)
    real_out = real_prod[:, :, 0] - imag_prod[:, :, 1]
    imag_out = real_prod[:, :, 1] + imag_prod[:, :, 0]
    return jnp.stack([real_out, imag_out], axis=2)


def inverse_rows(row_real, row_imag, packed_grad, col_back, source_count, col_count):
    real_prod = jnp.dot(row_real, packed_grad, preferred_element_type=jnp.float32)
    imag_prod = jnp.dot(row_imag, packed_grad, preferred_element_type=jnp.float32)
    real_prod = real_prod.reshape(real_prod.shape[0], source_count, 2, col_count)
    imag_prod = imag_prod.reshape(imag_prod.shape[0], source_count, 2, col_count)
    real_out = real_prod[:, :, 0] + imag_prod[:, :, 1]
    imag_out = real_prod[:, :, 1] - imag_prod[:, :, 0]
    joined = jnp.concatenate([real_out, imag_out], axis=-1).astype(jnp.bfloat16)
    result = jnp.dot(
        joined.reshape(-1, 2 * col_count), col_back, preferred_element_type=jnp.float32
    )
    return result.reshape(real_prod.shape[0], source_count, col_count)


def block_gradient(fourier, data_block, beam_block, mix_block, level_block):
    predicted = jnp.einsum("ct,ktzl->kczl", mix_block, fourier)
    beam_gain = beam_block.astype(jnp.float32)[:, :, None, :]
    residual = data_block.astype(jnp.float32) - beam_gain * predicted
    weight = level_block.astype(jnp.float32) * 0.25
    weighted = weight[None, :, None, None] * beam_gain * residual
    summed = jnp.einsum("cs,kczl->kszl", mix_block, weighted)
    return summed.astype(jnp.bfloat16)


def smooth_rows(padded, spacing, row_count):
    return (
        padded[0:row_count]
        + 2.0 * padded[spacing : spacing + row_count]
        + padded[2 * spacing : 2 * spacing + row_count]
    ) * 0.25


def smooth_cols(values, spacing):
    padded = jnp.pad(values, ((0, 0), (0, 0), (spacing, spacing)))
    return (
        padded[..., : -2 * spacing]
        + 2.0 * padded[..., spacing:-spacing]
        + padded[..., 2 * spacing :]
    ) * 0.25


def shrink(values, bound_value):
    return values - jnp.clip(values, -bound_value, bound_value)


def combine_scales(updated, smooth_one, coarse, fine_bound, coarse_bound):
    return (
        coarse
        + shrink(smooth_one - coarse, coarse_bound)
        + shrink(updated - smooth_one, fine_bound)
    )


def plain_body(sky_data, beam_gains, mixing, noise_levels, threshold_levels, start_sources):
    strip_rows, source_count, col_count = start_sources.shape
    full_rows = strip_rows * lax.axis_size("chan")
    row_real, row_imag = dft_tables(full_rows)
    col_real, col_imag = dft_tables(col_count)
    col_cat = jnp.concatenate([col_real, col_imag], axis=1)
    col_back = jnp.concatenate([col_real, col_imag], axis=0)
    bounds = threshold_levels.astype(jnp.float32) * 0.05
    fine_bound = bounds[:, 0][:, None]
    coarse_bound = bounds[:, 1][:, None]
    sources = start_sources
    for iteration in range(ITERS):
        rounded = sources.astype(jnp.bfloat16)
        gathered = lax.all_gather(rounded, "chan", axis=0, tiled=True)
        packed = column_part(gathered, col_cat)
        fourier = combine_forward(
            jnp.dot(row_real, packed, preferred_element_type=jnp.float32),
            jnp.dot(row_imag, packed, preferred_element_type=jnp.float32),
            source_count,
            col_count,
        )
        grad_local = block_gradient(fourier, sky_data, beam_gains, mixing, noise_levels)
        packed_grad = grad_local.reshape(full_rows, source_count * 2 * col_count)
        gradient = lax.psum_scatter(
            inverse_rows(row_real, row_imag, packed_grad, col_back, source_count, col_count),
            "chan",
            scatter_dimension=0,
            tiled=True,
        )
        updated = sources + gradient
        fine_pad = padded_2(updated, (("chan", 0),), 1)
        smooth_one = smooth_cols(smooth_rows(fine_pad, 1, strip_rows), 1)
        coarse_pad = padded_2(smooth_one, (("chan", 0),), 2)
        coarse = smooth_cols(smooth_rows(coarse_pad, 2, strip_rows), 2)
        sources = combine_scales(updated, smooth_one, coarse, fine_bound, coarse_bound)
    return sources


BF16 = jnp.bfloat16
F32 = jnp.float32
VMEM_LIMIT = 56 * 1024 * 1024
PAIRS = [(s, t) for s in range(4) for t in range(s, 4)]
PAIR_OF = {}
for number, (first, second) in enumerate(PAIRS):
    PAIR_OF[first, second] = number
    PAIR_OF[second, first] = number


def host_tables(length):
    positions = np.arange(length)
    angles = (positions[:, None] * positions[None, :] % length) * (2.0 * math.pi / length)
    norm_factor = 1.0 / math.sqrt(length)
    return (
        (np.cos(angles) * norm_factor).astype(np.float32).astype(ml_dtypes.bfloat16),
        (-np.sin(angles) * norm_factor).astype(np.float32).astype(ml_dtypes.bfloat16),
    )


def smooth_window(x, first_row, row_total, fine, coarse_bound):
    height, width = x.shape
    rows = lax.broadcasted_iota(jnp.int32, (height, width), 0) + first_row
    lanes = lax.broadcasted_iota(jnp.int32, (height, width), 1)
    inside = (rows >= 0) & (rows < row_total)

    def smooth(v, d):
        v = 0.25 * (pltpu.roll(v, d, 0) + 2.0 * v + pltpu.roll(v, height - d, 0))
        left = jnp.where(lanes >= d, pltpu.roll(v, d, 1), 0.0)
        right = jnp.where(lanes < width - d, pltpu.roll(v, width - d, 1), 0.0)
        return 0.25 * (left + 2.0 * v + right)

    c1 = jnp.where(inside, smooth(x, 1), 0.0)
    c2 = smooth(c1, 2)
    d1 = c1 - c2
    d0 = x - c1
    result = c2 + (d1 - jnp.clip(d1, -coarse_bound, coarse_bound)) + (d0 - jnp.clip(d0, -fine, fine))
    return result[8 : height - 8]


class Place:
    def __init__(self):
        self.me = me = lax.axis_index("chan")
        self.z, self.y, self.c = z, y, c = me // 4, (me // 2) % 2, me % 2
        self.core_peer = self.index(z, y, 1 - c)
        self.y_peer = self.index(z, 1 - y, c)
        self.z_peers = [self.index((z + 1 + i) % 4, y, c) for i in range(3)]
        self.peers = [self.core_peer, self.y_peer] + self.z_peers

    def index(self, z, y, c):
        return z * 4 + y * 2 + c

    def remote(self, src, dst, send, recv, peer):
        return pltpu.make_async_remote_copy(
            src_ref=src, dst_ref=dst, send_sem=send, recv_sem=recv,
            device_id={"chan": peer}, device_id_type=pl.DeviceIdType.MESH,
        )

    def greet(self, peers):
        barrier = pltpu.get_barrier_semaphore()
        for peer in peers:
            pl.semaphore_signal(barrier, inc=1, device_id={"chan": peer}, device_id_type=pl.DeviceIdType.MESH)

    def gather(self, buf, gz_s, gz_r, gy_s, gy_r, gc_s, gc_r):
        z, y, c = self.z, self.y, self.c
        held = [self.index((z + 4 - j) % 4, y, c) for j in range(4)]
        crossed = [self.index((z + 4 - j) % 4, 1 - y, c) for j in range(4)]

        def send(block, s_sem, r_sem, peer):
            return self.remote(buf.at[block], buf.at[block], s_sem, r_sem, peer)

        gz = [send(held[0], gz_s.at[i], gz_r.at[i], self.z_peers[i]) for i in range(3)]
        gy = [send(held[j], gy_s.at[j], gy_r.at[j], self.y_peer) for j in range(4)]
        gc = [send(block, gc_s.at[j], gc_r.at[j], self.core_peer) for j, block in enumerate(held + crossed)]
        return gz, gy, gc


def steps_kernel(
    s_ref, start_ref, d_ref, h_ref, colcat_ref, colback_ref, fwd_ref, bwd_ref, level_ref, out_ref,
    fwd_half, bwd_half, load, got_d, got_h, dsum_ref, hsum_ref, qst, pst, gst, vb, got_core, acc, got_y, fin, got_z, sall, own, xpad, halo,
    core_s, core_r, y_s, y_r, z_s, z_r, gz_s, gz_r, gy_s, gy_r, gc_s, gc_r, halo_s, halo_r, half_s, half_r,
):
    blocks, sources, strip, cols = s_ref.shape
    nrow = blocks * strip
    place = Place()
    me, z, y, c = place.me, place.z, place.y, place.c
    remote = place.remote
    right, left = (me + 1) % blocks, (me + blocks - 1) % blocks
    greeted = place.peers + [left, right]
    place.greet(greeted)

    half_k = nrow // 2
    mine_k = pl.multiple_of(c * nrow, nrow)
    keep_k = pl.ds(pl.multiple_of(c * half_k, half_k), half_k)
    load_fwd = pltpu.make_async_copy(fwd_ref.at[pl.ds(mine_k, nrow), :], fwd_half, load.at[0])
    load_h = pltpu.make_async_copy(h_ref.at[:, keep_k, :], hsum_ref, load.at[1])
    load_d = pltpu.make_async_copy(d_ref.at[:, :, keep_k, :], dsum_ref, load.at[2])
    load_bwd = pltpu.make_async_copy(bwd_ref.at[:, pl.ds(mine_k, nrow)], bwd_half, load.at[3])
    for copy in (load_fwd, load_h, load_d, load_bwd):
        copy.start()
    pl.semaphore_wait(pltpu.get_barrier_semaphore(), len(greeted))

    other = pl.ds(pl.multiple_of((1 - c) * half_k, half_k), half_k)
    swap_d = remote(d_ref.at[:, :, other, :], got_d, half_s.at[0], half_r.at[0], place.core_peer)
    swap_h = remote(h_ref.at[:, other, :], got_h, half_s.at[1], half_r.at[1], place.core_peer)
    swap_d.start()
    swap_h.start()
    for s in range(sources):
        own[s] = start_ref[:, s, :]

    def bound(s, j):
        return level_ref[s, j].astype(F32) * 0.05

    tile = 128
    thin = 16
    for iteration in range(ITERS):
        first, last = iteration == 0, iteration == ITERS - 1
        now_ref = s_ref if first else sall

        for t in range(sources):
            p = jnp.dot(now_ref[:, t].reshape(nrow, cols), colcat_ref[...], preferred_element_type=F32)
            pst[0:nrow, t * cols : (t + 1) * cols] = p[:, :cols].astype(BF16)
            pst[nrow:, t * cols : (t + 1) * cols] = p[:, cols:].astype(BF16)

            if first and t == 0:
                load_fwd.wait()
            block = slice(t * cols, (t + 1) * cols)
            qst[:, block] = jnp.dot(fwd_half[...], pst[:, block], preferred_element_type=F32)

        if first:
            load_h.wait()
            load_d.wait()
            swap_d.wait()
            swap_h.wait()

        @pl.loop(0, half_k // thin)
        def _(kb):
            k0 = pl.multiple_of(kb * thin, thin)
            here = pl.ds(k0, thin)
            if first:
                h = [(hsum_ref[p, here, :].astype(F32) + got_h[p, here, :].astype(F32)) for p in range(len(PAIRS))]
                for p in range(len(PAIRS)):
                    hsum_ref[p, here, :] = h[p].astype(BF16)
            else:
                h = [hsum_ref[p, here, :].astype(F32) for p in range(len(PAIRS))]
            for part in range(2):
                rows = pl.ds(pl.multiple_of(part * half_k + k0, thin), thin)
                q = [qst[rows, t * cols : (t + 1) * cols] for t in range(sources)]
                for s in range(sources):
                    if first:
                        g = dsum_ref[part, s, here, :].astype(F32) + got_d[part, s, here, :].astype(F32)
                        dsum_ref[part, s, here, :] = g.astype(BF16)
                    else:
                        g = dsum_ref[part, s, here, :].astype(F32)
                    for t in range(sources):
                        g = g - h[PAIR_OF[s, t]] * q[t]
                    gst[rows, s * cols : (s + 1) * cols] = g.astype(BF16)

        core_copies, y_copies, z_copies = [], [], []

        def do_core(i):
            zb = (z + 1 + i) % 4
            rows = pl.ds(pl.multiple_of(2 * zb * tile, 2 * tile), 2 * tile)
            u = jnp.dot(bwd_half[rows, :], gst[...], preferred_element_type=F32).astype(BF16)
            both = [u[:, s * cols : (s + 1) * cols] for s in range(sources)]
            both = [jnp.concatenate([part[:tile], part[tile:]], axis=1) for part in both]
            v = jnp.dot(jnp.concatenate(both, axis=0), colback_ref[...], preferred_element_type=F32).astype(BF16)
            for s in range(sources):
                vb[i, :, :, s] = v[s * tile : (s + 1) * tile].reshape(2, 2, strip, cols)
            copy = remote(vb.at[i, :, 1 - c], got_core.at[i], core_s.at[i], core_r.at[i], place.core_peer)
            copy.start()
            core_copies.append(copy)

        def do_y(i):
            core_copies[i].wait()
            acc[i] = (vb[i, :, c].astype(F32) + got_core[i].astype(F32)).astype(BF16)
            copy = remote(acc.at[i, 1 - y], got_y.at[i], y_s.at[i], y_r.at[i], place.y_peer)
            copy.start()
            y_copies.append(copy)

        def do_z(i):
            y_copies[i].wait()
            fin[i] = (acc[i, y].astype(F32) + got_y[i].astype(F32)).astype(BF16)
            copy = remote(fin.at[i], got_z.at[i], z_s.at[i], z_r.at[i], place.z_peers[i])
            copy.start()
            z_copies.append(copy)

        if first:
            load_bwd.wait()
        do_core(0)
        do_core(1)
        do_y(0)
        do_core(2)
        do_y(1)
        do_z(0)
        do_core(3)
        do_y(2)
        do_z(1)
        do_y(3)
        do_z(2)
        y_copies[3].wait()
        total = own[...] + (acc[3, y].astype(F32) + got_y[3].astype(F32))
        for i in range(3):
            z_copies[i].wait()
            total = total + got_z[i].astype(F32)

        xpad[:, 8 : 8 + strip] = total
        to_right = remote(xpad.at[:, strip : strip + 8], halo.at[0], halo_s.at[0], halo_r.at[0], right)
        to_left = remote(xpad.at[:, 8:16], halo.at[1], halo_s.at[1], halo_r.at[1], left)
        to_right.start()
        to_left.start()
        to_right.wait()
        to_left.wait()
        xpad[:, 0:8] = jnp.where(me > 0, halo[0], 0.0)
        xpad[:, 8 + strip : 16 + strip] = jnp.where(me < blocks - 1, halo[1], 0.0)
        for s in range(sources):
            result = smooth_window(xpad[s], me * strip - 8, nrow, bound(s, 0), bound(s, 1))
            if last:
                out_ref[:, s, :] = result
            else:
                own[s] = result
                sall[me, s] = result.astype(BF16)

        if not last:
            gz, gy, gc = place.gather(sall, gz_s, gz_r, gy_s, gy_r, gc_s, gc_r)
            for copy in gz + [gy[0], gc[0]]:
                copy.start()
            for j in range(1, 4):
                gz[j - 1].wait_recv()
                gy[j].start()
                gc[j].start()
            for j in range(4):
                gy[j].wait_recv()
                gc[4 + j].start()
            for copy in gc:
                copy.wait_recv()
            for copy in gz + gy + gc:
                copy.wait_send()


def steps(s_full, start, dd, hh, tables, levels):
    blocks, sources, strip, cols = s_full.shape
    nrow = blocks * strip
    vm, hbm = pl.BlockSpec(memory_space=pltpu.VMEM), pl.BlockSpec(memory_space=pl.ANY)
    dma = pltpu.SemaphoreType.DMA
    block = (sources, strip, cols)
    sum_d = (2, sources, nrow // 2, cols)
    sum_h = (len(PAIRS), nrow // 2, cols)
    return pl.pallas_call(
        steps_kernel,
        out_shape=jax.ShapeDtypeStruct(start.shape, F32),
        in_specs=[vm] * 2 + [hbm] * 2 + [vm] * 2 + [hbm] * 2 + [pl.BlockSpec(memory_space=pltpu.SMEM)],
        out_specs=vm,
        scratch_shapes=[
            pltpu.VMEM((nrow, 2 * nrow), BF16),
            pltpu.VMEM((2 * nrow, nrow), BF16),
            dma((4,)),
            pltpu.VMEM(sum_d, BF16),
            pltpu.VMEM(sum_h, BF16),
            pltpu.VMEM(sum_d, BF16),
            pltpu.VMEM(sum_h, BF16),
            pltpu.VMEM((nrow, sources * cols), F32),
            pltpu.VMEM((2 * nrow, sources * cols), BF16),
            pltpu.VMEM((nrow, sources * cols), BF16),
            pltpu.VMEM((4, 2, 2) + block, BF16),
            pltpu.VMEM((4, 2) + block, BF16),
            pltpu.VMEM((4, 2) + block, BF16),
            pltpu.VMEM((4,) + block, BF16),
            pltpu.VMEM((3,) + block, BF16),
            pltpu.VMEM((3,) + block, BF16),
            pltpu.VMEM((blocks,) + block, BF16),
            pltpu.VMEM(block, F32),
            pltpu.VMEM((sources, strip + 16, cols), F32),
            pltpu.VMEM((2, sources, 8, cols), F32),
            dma((4,)), dma((4,)), dma((4,)), dma((4,)), dma((3,)), dma((3,)),
            dma((3,)), dma((3,)), dma((4,)), dma((4,)), dma((8,)), dma((8,)),
            dma((2,)), dma((2,)), dma((2,)), dma((2,)),
        ],
        compiler_params=pltpu.CompilerParams(collective_id=0, has_side_effects=True, vmem_limit_bytes=VMEM_LIMIT),
    )(s_full, start, dd, hh, *tables, levels)


def sums_kernel(start_ref, d_ref, g_ref, mix_ref, level_ref, expand_ref, copy_d_ref, copy_h_ref, mask_d_ref, mask_h_ref,
                dd_ref, hh_ref, s_ref, wd_ref, wh_ref, own, own_sem, *gather_sems):
    at = pl.program_id(0)
    place = Place()
    gz, gy, gc = place.gather(s_ref, *gather_sems)
    keep = pltpu.make_async_copy(own, s_ref.at[place.me], own_sem)

    @pl.when(at == 0)
    def _():
        place.greet(place.peers)
        for s in range(4):
            own[s] = start_ref[:, s, :].astype(BF16)
        keep.start()

    @pl.when(at == 1)
    def _():
        keep.wait()
        pl.semaphore_wait(pltpu.get_barrier_semaphore(), len(place.peers))
        for copy in gz + [gy[0], gc[0]]:
            copy.start()

    @pl.when(at == 5)
    def _():
        for j in range(1, 4):
            gz[j - 1].wait_recv()
            gy[j].start()
            gc[j].start()

    @pl.when(at == 9)
    def _():
        for j in range(4):
            gy[j].wait_recv()
            gc[4 + j].start()

    @pl.when(at == pl.num_programs(0) - 1)
    def _():
        for copy in gc:
            copy.wait_recv()
        for copy in gz + gy + gc:
            copy.wait_send()

    @pl.when(pl.program_id(0) == 0)
    def _():
        mix = mix_ref[...]
        weighted = mix * (level_ref[...].astype(F32) * 0.25)
        chans = mix.shape[1]
        by_source = [jnp.broadcast_to(weighted[s : s + 1], (16, chans)) for s in range(4)]
        by_pair = [jnp.broadcast_to(weighted[s : s + 1] * mix[t : t + 1], (8, chans)) for s, t in PAIRS]
        wd = jnp.concatenate(by_source + by_source, axis=0).astype(BF16)
        wh = jnp.concatenate(by_pair, axis=0).astype(BF16)
        wd = jnp.dot(wd, copy_d_ref[...], preferred_element_type=F32) * mask_d_ref[...].astype(F32)
        wh = jnp.dot(wh, copy_h_ref[...], preferred_element_type=F32) * mask_h_ref[...].astype(F32)
        wd_ref[...] = wd.astype(BF16)
        wh_ref[...] = wh.astype(BF16)

    groups = g_ref.shape[0] // 16
    chans, cols = g_ref.shape[1:]
    wide = 4 * chans
    half = cols // 2
    for n in range(groups):
        products = []
        for j in range(8):
            ks = (16 * n + j, 16 * n + 8 + j)
            pair = [jnp.concatenate([g_ref[k, :, :half], g_ref[k, :, half:]], axis=0) for k in ks]
            spread = jnp.dot(expand_ref[...], jnp.concatenate(pair, axis=1), preferred_element_type=F32)
            d = jnp.concatenate([d_ref[k * wide : (k + 1) * wide, :] for k in ks], axis=1)
            products.append(d * spread.astype(BF16))
        total = jnp.dot(wd_ref[...], jnp.concatenate(products, axis=0), preferred_element_type=F32)
        for r in range(16):
            z, s, lt = r // 8, r // 2 % 4, r % 2
            rows = total[8 * r : 8 * r + 8]
            both = jnp.concatenate([rows[:, :half], rows[:, half:]], axis=0)
            dd_ref[z, s, 16 * n : 16 * n + 16, lt * half : (lt + 1) * half] = both.astype(BF16)
        grams = []
        for k in (16 * n, 16 * n + 8):
            squares = (g_ref[k : k + 8] * g_ref[k : k + 8]).reshape(8 * chans, cols)
            grams.append(jnp.dot(wh_ref[...], squares, preferred_element_type=F32))
        for p in range(len(PAIRS)):
            both = jnp.concatenate([gram[8 * p : 8 * p + 8] for gram in grams], axis=0)
            hh_ref[p, 16 * n : 16 * n + 16, :] = both.astype(BF16)


def channel_sums(sky_data, beam_gains, mixing, noise_levels, start):
    nrow, chans, _, cols = sky_data.shape
    strip, sources, _ = start.shape
    blocks = nrow // strip
    dma = pltpu.SemaphoreType.DMA
    half = cols // 2
    ones = np.ones
    eye = np.eye
    mask_d = np.einsum("s,kK,lL,zZ,c->zslkKcLZ", ones(4), eye(8), eye(2), eye(2), ones(chans)).reshape(128, -1)
    mask_h = np.einsum("p,kK,c->pkKc", ones(len(PAIRS)), eye(8), ones(chans)).reshape(8 * len(PAIRS), -1)
    copy_d = np.einsum("cC,k,r->ckCr", eye(chans), ones(8), ones(4)).reshape(chans, -1)
    copy_h = np.einsum("cC,k->ckC", eye(chans), ones(8)).reshape(chans, -1)
    expand = np.einsum("cC,lL,z->clzLC", np.eye(chans), np.eye(2), np.ones(2)).reshape(4 * chans, 2 * chans)
    rows = jnp.swapaxes(sky_data.reshape(nrow, chans, 2, 2, half), 2, 3).reshape(-1, half)
    tile = 32
    tables = [jnp.asarray(t.astype(ml_dtypes.bfloat16)) for t in (expand, copy_d, copy_h, mask_d, mask_h)]
    return pl.pallas_call(
        sums_kernel,
        grid=(nrow // tile,),
        out_shape=(
            jax.ShapeDtypeStruct((2, 4, nrow, cols), BF16),
            jax.ShapeDtypeStruct((len(PAIRS), nrow, cols), BF16),
            jax.ShapeDtypeStruct((blocks, sources, strip, cols), BF16),
        ),
        in_specs=[
            pl.BlockSpec(start.shape, lambda i: (0, 0, 0)),
            pl.BlockSpec((tile * 4 * chans, half), lambda i: (i, 0)),
            pl.BlockSpec((tile, chans, cols), lambda i: (i, 0, 0)),
            pl.BlockSpec((4, chans), lambda i: (0, 0)),
            pl.BlockSpec((1, chans), lambda i: (0, 0)),
        ]
        + [pl.BlockSpec(table.shape, lambda i: (0, 0)) for table in tables],
        out_specs=(
            pl.BlockSpec((2, 4, tile, cols), lambda i: (0, 0, i, 0)),
            pl.BlockSpec((len(PAIRS), tile, cols), lambda i: (0, i, 0)),
            pl.BlockSpec(memory_space=pl.ANY),
        ),
        scratch_shapes=[
            pltpu.VMEM((128, 32 * chans), BF16),
            pltpu.VMEM((8 * len(PAIRS), 8 * chans), BF16),
            pltpu.VMEM((sources, strip, cols), BF16),
            dma, dma((3,)), dma((3,)), dma((4,)), dma((4,)), dma((8,)), dma((8,)),
        ],
        compiler_params=pltpu.CompilerParams(collective_id=1, has_side_effects=True, vmem_limit_bytes=VMEM_LIMIT),
        cost_estimate=pl.CostEstimate(flops=2 * 10**9, bytes_accessed=30 * 10**6, transcendentals=0),
    )(start, rows, beam_gains, mixing.T, noise_levels.reshape(1, chans), *tables)


def body(sky_data, beam_gains, mixing, noise_levels, threshold_levels, start_sources):
    strip, sources, cols = start_sources.shape
    blocks = lax.axis_size("chan")
    if blocks != 16 or strip != 32 or sources != 4 or cols != 256 or sky_data.shape[1] != 32:
        return plain_body(sky_data, beam_gains, mixing, noise_levels, threshold_levels, start_sources)
    row_real, row_imag = host_tables(strip * blocks)
    col_real, col_imag = host_tables(cols)
    forward = np.block([[row_real, -row_imag], [row_imag, row_real]])
    backward = np.block([[row_real, row_imag], [-row_imag, row_real]])
    quarter = strip * blocks // 4
    backward = backward.reshape(2, 4, quarter, -1).swapaxes(0, 1).reshape(8 * quarter, -1)
    half_k = strip * blocks // 2
    starts = [0, 2 * half_k, half_k, 3 * half_k]
    tables = [
        jnp.asarray(np.concatenate([col_real, col_imag], axis=1)),
        jnp.asarray(np.concatenate([col_real, col_imag], axis=0)),
        jnp.asarray(np.concatenate([forward[part : part + half_k] for part in starts], axis=0)),
        jnp.asarray(np.concatenate([backward[:, part : part + half_k] for part in starts], axis=1)),
    ]
    dd, hh, s_full = channel_sums(sky_data, beam_gains, mixing, noise_levels, start_sources)
    return steps(s_full, start_sources, dd, hh, tables, threshold_levels)


def solution(mesh):
    return jax.shard_map(
        body,
        mesh=mesh,
        in_specs=(
            P("groups", "chan", None, None),
            P("groups", "chan", None),
            P(("groups", "chan"), None),
            P("chan"),
            P(),
            P(("groups", "chan"), None, None),
        ),
        out_specs=P(("groups", "chan"), None, None),
        check_vma=False,
    )
```
